32 devices in a mesh: fsdp: 4 (over z), ctx: 4 (over y, x), tp: 2 (over core).
Axes of the slice: x: 2, y: 2, z: 4, core: 2. Of those that a mesh axis runs over, the one named last changes fastest.
Arguments:
- block_input: bfloat16 [4, 1024, 1024], P('fsdp', 'ctx'), may hold values from -6 to 6
- norm_gain: bfloat16 [1024], P('fsdp'), may hold values from 0.25 to 1.75
- w_xz: bfloat16 [1024, 2, 2048], P(None, None, ('fsdp', 'tp')), may hold values from -0.1875 to 0.1875
- w_bc: bfloat16 [1024, 256], P('fsdp'), may hold values from -0.1875 to 0.1875
- w_dt: bfloat16 [1024, 32], P(None, ('fsdp', 'tp')), may hold values from -0.1875 to 0.1875
- conv_x: bfloat16 [4, 2048], P(None, ('fsdp', 'tp')), may hold values from -3 to 3
- conv_bc: bfloat16 [4, 256], P(None, 'fsdp'), may hold values from -3 to 3
- conv_bias_x: bfloat16 [2048], P(('fsdp', 'tp')), may hold values from -0.5 to 0.5
- conv_bias_bc: bfloat16 [256], P('fsdp'), may hold values from -0.5 to 0.5
- dt_bias: bfloat16 [32], P(('fsdp', 'tp')), may hold values from -4 to -2
- a_log: bfloat16 [32], P(('fsdp', 'tp')), as said below
- d_skip: bfloat16 [32], P(('fsdp', 'tp')), may hold values from 0.5 to 1.5
- gate_gain: bfloat16 [2048], P(('fsdp', 'tp')), may hold values from 0.25 to 1.75
- w_out: bfloat16 [2048, 1024], P(('fsdp', 'tp')), may hold values from -0.125 to 0.125
- out_cotangent: bfloat16 [4, 1024, 1024], P('fsdp', 'ctx'), may hold values from -6 to 6
Outputs:
- block_out: bfloat16 [4, 1024, 1024], P('fsdp', 'ctx')
- input_grad: float32 [4, 1024, 1024], P('fsdp', 'ctx')
- grad_norm_gain: float32 [1024], P('fsdp')
- grad_w_xz: float32 [1024, 2, 2048], P(None, None, ('fsdp', 'tp'))
- grad_w_bc: float32 [1024, 256], P('fsdp')
- grad_w_dt: float32 [1024, 32], P(None, ('fsdp', 'tp'))
- grad_conv_x: float32 [4, 2048], P(None, ('fsdp', 'tp'))
- grad_conv_bc: float32 [4, 256], P(None, 'fsdp')
- grad_conv_bias_x: float32 [2048], P(('fsdp', 'tp'))
- grad_conv_bias_bc: float32 [256], P('fsdp')
- grad_dt_bias: float32 [32], P(('fsdp', 'tp'))
- grad_a_log: float32 [32], P(('fsdp', 'tp'))
- grad_d_skip: float32 [32], P(('fsdp', 'tp'))
- grad_gate_gain: float32 [2048], P(('fsdp', 'tp'))
- grad_w_out: float32 [2048, 1024], P(('fsdp', 'tp'))
The draws below stay inside these ranges and needn't reach their ends.
Inputs may be any that keep to these rules, and one draw needn't show every extreme that they name: exp(a_log) lies between 2 / 1024 and 1.
All inputs are finite; a program needn't handle non-finite values.
Results may differ from the reference program's by a relative error of at most 0.019.
Values may be sent and summed in bfloat16 or wider, within the bound.
A program may use at most 128 MiB of HBM per device.

```python
import math
import jax
import jax.numpy as jnp
from jax import lax

D = 1024
INNER = 2048
HEADS = 32
HEAD_DIM = 64
STATE = 128
CONV = 4
GROUP = 256
SEQS = 4
LENGTH = 1024


def draw_a_log(key, part):
    key = jax.random.fold_in(key, 7)
    pick_key, slow_key, fast_key = jax.random.split(key, 3)
    slow_share = 0.5
    is_slow = jax.random.uniform(pick_key, (HEADS,), jnp.float32) < slow_share
    slow_rate = jnp.exp(jax.random.uniform(slow_key, (HEADS,), jnp.float32, math.log(2.0), math.log(25.0))) / LENGTH
    fast_rate = jnp.exp(jax.random.uniform(fast_key, (HEADS,), jnp.float32, math.log(0.3), math.log(1.0)))
    return jnp.log(jnp.where(is_slow, slow_rate, fast_rate)).astype(jnp.bfloat16)


def block_scale(own_key, dims, cuts, least, top_value):
    def one(axis_at, blocks):
        draws = jax.random.uniform(jax.random.fold_in(jax.random.fold_in(own_key, 6), axis_at), (blocks,), jnp.float32, least / len(cuts), top_value / len(cuts))
        return jnp.repeat(jnp.exp(draws), dims[axis_at] // blocks).reshape((-1,) + (1,) * (len(dims) - axis_at - 1))

    loudness = one(*cuts[0])
    for cut in cuts[1:]:
        loudness = loudness * one(*cut)
    return loudness


def normal_values(stream_key, shape, deviation, bound, shards=(), kind=jnp.bfloat16):
    array = jax.random.normal(stream_key, shape, jnp.float32) * deviation
    if len(shards) > 0:
        array = block_scale(stream_key, shape, shards, -0.22, 0.18) * array
    return jnp.clip(array, min=-bound, max=bound).astype(kind)


def setup_inputs(seed: int = 0) -> dict:
    keys = jax.random.split(jax.random.key(seed), 16)
    return {
        "block_input": normal_values(keys[0], (SEQS, LENGTH, D), 1.0, 6.0, ((0, 4), (1, 4))),
        "norm_gain": jnp.clip(1.0 + 0.15 * jax.random.normal(keys[1], (D,), jnp.float32), 0.25, 1.75).astype(jnp.bfloat16),
        "w_xz": normal_values(keys[2], (D, 2, INNER), D ** -0.5, 0.1875, ((2, 8),)),
        "w_bc": normal_values(keys[3], (D, 2 * STATE), D ** -0.5, 0.1875, ((0, 4),)),
        "w_dt": normal_values(keys[4], (D, HEADS), D ** -0.5, 0.1875, ((1, 8),)),
        "conv_x": normal_values(keys[5], (CONV, INNER), CONV ** -0.5, 3.0, ((1, 8),)),
        "conv_bc": normal_values(keys[6], (CONV, 2 * STATE), CONV ** -0.5, 3.0, ((1, 4),)),
        "conv_bias_x": jnp.clip(jax.random.uniform(keys[7], (INNER,), jnp.float32, -0.5, 0.5) * block_scale(keys[7], (INNER,), ((0, 8),), -0.4, 0.0), -0.5, 0.5).astype(jnp.bfloat16),
        "conv_bias_bc": jnp.clip(jax.random.uniform(keys[8], (2 * STATE,), jnp.float32, -0.5, 0.5) * block_scale(keys[8], (2 * STATE,), ((0, 4),), -0.4, 0.0), -0.5, 0.5).astype(jnp.bfloat16),
        "dt_bias": jnp.clip(-4.0 + 2.0 * jax.random.uniform(keys[9], (HEADS,), jnp.float32) ** block_scale(keys[9], (HEADS,), ((0, 8),), -0.2, 0.2), -4.0, -2.0).astype(jnp.bfloat16),
        "a_log": draw_a_log(jax.random.fold_in(keys[15], 71), 0),
        "d_skip": jnp.clip(0.5 + 1.0 * jax.random.uniform(keys[11], (HEADS,), jnp.float32) ** block_scale(keys[11], (HEADS,), ((0, 8),), -0.2, 0.2), 0.5, 1.5).astype(jnp.bfloat16),
        "gate_gain": jnp.clip(1.0 + 0.15 * jax.random.normal(keys[12], (INNER,), jnp.float32), 0.25, 1.75).astype(jnp.bfloat16),
        "w_out": normal_values(keys[13], (INNER, D), INNER ** -0.5, 0.125, ((0, 8),)),
        "out_cotangent": normal_values(keys[14], (SEQS, LENGTH, D), 1.0, 6.0, ((0, 4), (1, 4))),
    }


EPSILON = 1e-05
PRECISE = lax.Precision.HIGHEST

@jax.custom_vjp
def low(v):
    return lax.optimization_barrier(v.astype(jnp.bfloat16)).astype(jnp.float32)

@jax.custom_vjp
def low_back(v):
    return v

def low_keep(v):
    return (low(v), None)

def low_pass(kept, grad):
    return (grad,)

def back_keep(v):
    return (v, None)

def back_low(kept, grad):
    return (low(grad),)
low.defvjp(low_keep, low_pass)
low_back.defvjp(back_keep, back_low)

def pre_norm(values, gain):
    mean_sq = lax.optimization_barrier(jnp.mean(values * values, -1, keepdims=True))
    return values * lax.rsqrt(mean_sq + EPSILON) * gain

def conv_silu(extended, taps_w, taps_b):
    tap_count = taps_w.shape[0]
    out_rows = extended.shape[1] - tap_count + 1
    running = taps_b + extended[:, 0:out_rows] * taps_w[0]
    for offset in range(1, tap_count):
        running = running + extended[:, offset:offset + out_rows] * taps_w[offset]
    return jax.nn.silu(running)

def ssd_local(x_heads, b_mat, c_mat, dt_raw, dt_bias, a_log, d_skip):
    step_size = jax.nn.softplus(dt_raw + dt_bias)
    log_decay = -step_size * jnp.exp(a_log)
    cumul = jnp.cumsum(log_decay, axis=1)
    across = jnp.transpose(cumul, (0, 2, 1))
    step_t = jnp.transpose(step_size, (0, 2, 1))
    block_len = x_heads.shape[1]
    later_pos = lax.broadcasted_iota(jnp.int32, (block_len, block_len), 0)
    earlier_pos = lax.broadcasted_iota(jnp.int32, (block_len, block_len), 1)
    causal = later_pos >= earlier_pos
    gaps = across[:, :, :, None] - across[:, :, None, :]
    kernel = jnp.exp(jnp.where(causal, gaps, -1e+30))
    scores = jnp.einsum('sln,smn->slm', c_mat, b_mat, precision=PRECISE)
    mixing = scores[:, None] * kernel * step_t[:, :, None, :]
    y_loc = jnp.einsum('shlm,smhp->slhp', mixing, x_heads, precision=PRECISE) + d_skip[:, None] * x_heads
    final = across[:, :, -1:]
    carry_w = jnp.exp(final - across) * step_t
    scaled = x_heads * jnp.transpose(carry_w, (0, 2, 1))[..., None]
    s_loc = jnp.einsum('slhp,sln->shpn', scaled, b_mat, precision=PRECISE)
    return (y_loc, jnp.exp(cumul), jnp.exp(final[..., 0]), s_loc)

def state_read(c_mat, growth, s_in):
    reading = jnp.einsum('sln,shpn->slhp', c_mat, s_in, precision=PRECISE)
    return growth[..., None] * reading

def block_sequence(inputs, params):
    norm_gain, w_xz, w_bc, w_dt, conv_x, conv_bc, conv_bias_x, conv_bias_bc, dt_bias, a_log, d_skip, gate_gain, w_out = params
    seq_len = inputs.shape[0]
    blocks = seq_len // GROUP
    normed = low(pre_norm(inputs, norm_gain))
    proj_xz = jnp.einsum('ld,dke->lke', normed, w_xz, precision=PRECISE)
    proj_bc = jnp.dot(normed, w_bc, precision=PRECISE)
    dt_raw = low_back(jnp.dot(normed, w_dt, precision=PRECISE))
    gate_in = low_back(proj_xz[:, 1])
    conv_in = low(low_back(jnp.concatenate([proj_xz[:, 0], proj_bc], -1)))
    padded = jnp.pad(conv_in, ((CONV - 1, 0), (0, 0)))[None]
    conv_w = jnp.concatenate([conv_x, conv_bc], -1)
    conv_b = jnp.concatenate([conv_bias_x, conv_bias_bc], -1)
    mixed = low(conv_silu(padded, conv_w, conv_b)[0])
    x_heads = mixed[:, :INNER].reshape(blocks, GROUP, HEADS, HEAD_DIM)
    b_mat = mixed[:, INNER:INNER + STATE].reshape(blocks, GROUP, STATE)
    c_mat = mixed[:, INNER + STATE:].reshape(blocks, GROUP, STATE)
    y_loc, growth, decay, s_loc = ssd_local(x_heads, b_mat, c_mat, dt_raw.reshape(blocks, GROUP, HEADS), dt_bias, a_log, d_skip)

    def advance(carried, element):
        return (element[0][:, None, None] * carried + element[1], carried)
    unused, s_in = lax.scan(advance, jnp.zeros(s_loc.shape[1:], jnp.float32), (decay, s_loc))
    y_all = (y_loc + state_read(c_mat, growth, s_in)).reshape(seq_len, INNER)
    gated = y_all * jax.nn.silu(gate_in)
    scale = lax.rsqrt(lax.optimization_barrier(jnp.mean(gated * gated, -1, keepdims=True)) + EPSILON)
    normed_out = low(gated * scale * gate_gain)
    return inputs + jnp.dot(normed_out, w_out, precision=PRECISE)

def forward(inputs_all, params):
    checked = jax.checkpoint(block_sequence)

    def one_sequence(sequence):
        return checked(sequence, params)
    return lax.map(one_sequence, inputs_all)

def reference(block_input, norm_gain, w_xz, w_bc, w_dt, conv_x, conv_bc, conv_bias_x, conv_bias_bc, dt_bias, a_log, d_skip, gate_gain, w_out, out_cotangent):
    params = (norm_gain.astype(jnp.float32), w_xz.astype(jnp.float32), w_bc.astype(jnp.float32), w_dt.astype(jnp.float32), conv_x.astype(jnp.float32), conv_bc.astype(jnp.float32), conv_bias_x.astype(jnp.float32), conv_bias_bc.astype(jnp.float32), dt_bias.astype(jnp.float32), a_log.astype(jnp.float32), d_skip.astype(jnp.float32), gate_gain.astype(jnp.float32), w_out.astype(jnp.float32))
    inputs = block_input.astype(jnp.float32)
    result, pullback = jax.vjp(forward, inputs, params)
    input_grad, grads = pullback(out_cotangent.astype(jnp.float32))
    return (result.astype(jnp.bfloat16), input_grad, grads[0], grads[1], grads[2], grads[3], grads[4], grads[5], grads[6], grads[7], grads[8], grads[9], grads[10], grads[11], grads[12])
```

```python
import jax
import jax.numpy as jnp
from jax import lax
from jax.sharding import PartitionSpec as P

EPSILON = 1e-05
PRECISE = lax.Precision.DEFAULT


def shifted(value, axis, steps):
    count = lax.axis_size(axis)
    initial, last = (max(0, -steps), min(count, count - steps))
    return lax.ppermute(value, axis, [(source, source + steps) for source in range(initial, last)])


def entering_2(x, axis, combine, identity):
    count, place = (lax.axis_size(axis), lax.axis_index(axis))
    everything = jax.tree.map(
        lambda part, kind: lax.all_gather(part.astype(kind), axis), x, (jnp.bfloat16, jnp.bfloat16)
    )
    start = jax.tree.map(
        lambda part, zero: jnp.broadcast_to(jnp.asarray(zero, part.dtype), part.shape), x, identity
    )

    def hop(k, before):
        reached = k < place
        new = combine(
            before, jax.tree.map(lambda part, own: part[k].astype(own.dtype), everything, x)
        )
        return jax.tree.map(lambda a, b: jnp.where(reached, a, b), new, before)

    return lax.fori_loop(0, count, hop, start)


def entering_3(x, axis, join, neutral):
    count = lax.axis_size(axis)
    place = lax.axis_index(axis)
    ahead = count - 1 - place
    gathered = jax.tree.map(
        lambda a, kind: lax.all_gather(a.astype(kind), axis),
        x,
        jax.tree.map(lambda a: jnp.bfloat16 if a.dtype == jnp.float32 else a.dtype, x),
    )
    state = jax.tree.map(lambda a, e: jnp.zeros_like(a) + jnp.asarray(e, a.dtype), x, neutral)

    def one(hop, state):
        source = count - 1 - hop
        return join(
            state,
            jax.tree.map(
                lambda a, own: lax.dynamic_index_in_dim(a, source, 0, False).astype(own.dtype),
                gathered,
                x,
            ),
        )

    return lax.fori_loop(0, ahead, one, state)


def pre_norm(values, gain):
    mean_sq = jnp.mean(values * values, -1, keepdims=True)
    return values * lax.rsqrt(mean_sq + EPSILON) * gain


def conv_silu(extended, taps_w, taps_b):
    tap_count = taps_w.shape[0]
    out_rows = extended.shape[1] - tap_count + 1
    running = taps_b + extended[:, 0:out_rows] * taps_w[0]
    for offset in range(1, tap_count):
        running = running + extended[:, offset : offset + out_rows] * taps_w[offset]
    return jax.nn.silu(running)


def ssd_local(x_heads, b_mat, c_mat, dt_raw, dt_bias, a_log, d_skip):
    step_size = jax.nn.softplus(dt_raw + dt_bias)
    log_decay = -step_size * jnp.exp(a_log)
    cumul = jnp.cumsum(log_decay, axis=1)
    across = jnp.transpose(cumul, (0, 2, 1))
    step_t = jnp.transpose(step_size, (0, 2, 1))
    block_len = x_heads.shape[1]
    later_pos = lax.broadcasted_iota(jnp.int32, (block_len, block_len), 0)
    earlier_pos = lax.broadcasted_iota(jnp.int32, (block_len, block_len), 1)
    causal = later_pos >= earlier_pos
    gaps = across[:, :, :, None] - across[:, :, None, :]
    kernel = jnp.exp(jnp.where(causal, gaps, -1e30))
    scores = jnp.einsum("sln,smn->slm", c_mat, b_mat, precision=PRECISE)
    mixing = scores[:, None] * kernel * step_t[:, :, None, :]
    y_loc = (
        jnp.einsum("shlm,smhp->slhp", mixing, x_heads, precision=PRECISE)
        + d_skip[:, None] * x_heads
    )
    final = across[:, :, -1:]
    carry_w = jnp.exp(final - across) * step_t
    scaled = x_heads * jnp.transpose(carry_w, (0, 2, 1))[..., None]
    s_loc = jnp.einsum("slhp,sln->shpn", scaled, b_mat, precision=PRECISE)
    return (y_loc, jnp.exp(cumul), jnp.exp(final[..., 0]), s_loc)


def state_read(c_mat, growth, s_in):
    reading = jnp.einsum("sln,shpn->slhp", c_mat, s_in, precision=PRECISE)
    return growth[..., None] * reading


def chain_step(earlier, later):
    return (earlier[0] * later[0], earlier[1] * later[0][:, :, None, None] + later[1])


def pad_rows(parts, width, multiple):
    flat = jnp.concatenate([part.reshape(-1) for part in parts])
    unit = width * multiple
    total = -(-flat.shape[0] // unit) * unit
    return jnp.pad(flat, (0, total - flat.shape[0])).reshape(-1, width)


def unpack(flat, shapes):
    out, at = [], 0
    for shape in shapes:
        size = 1
        for n in shape:
            size *= n
        out.append(flat[..., at : at + size].reshape(flat.shape[:-1] + tuple(shape)))
        at += size
    return out


def gather_rows(x):
    half = x.shape[0] // lax.axis_size("tp")
    mine = lax.dynamic_slice_in_dim(x, lax.axis_index("tp") * half, half, 0)
    full = lax.all_gather(mine, ("fsdp", "tp"))
    return full.reshape((lax.axis_size("fsdp"),) + x.shape)


def scatter_sum(x):
    part = lax.psum_scatter(x, "fsdp", scatter_dimension=0, tiled=False)
    return lax.psum(part, "tp")


def body(
    block_input,
    norm_gain,
    w_xz,
    w_bc,
    w_dt,
    conv_x,
    conv_bc,
    conv_bias_x,
    conv_bias_bc,
    dt_bias,
    a_log,
    d_skip,
    gate_gain,
    w_out,
    out_cotangent,
):
    f32, low = jnp.float32, jnp.bfloat16
    groups = lax.axis_size("fsdp")
    own = lax.axis_index("fsdp")
    seq_own, rows, width = block_input.shape
    own_rows = seq_own * rows
    seqs = groups * seq_own
    tokens = seqs * rows
    inner = w_xz.shape[2]
    inner_total = inner * groups * lax.axis_size("tp")
    maps = w_bc.shape[1]
    state = maps // 2
    heads = w_dt.shape[1]
    head_size = inner // heads
    taps = conv_x.shape[0]
    edge = taps - 1

    small_shapes = (w_bc.shape, norm_gain.shape, conv_bc.shape, conv_bias_bc.shape)
    small = pad_rows((w_bc, norm_gain, conv_bc, conv_bias_bc), width, 32)
    x_own = block_input.reshape(own_rows, width)
    packed = gather_rows(jnp.concatenate([x_own, small], 0))
    cot_low = gather_rows(out_cotangent.reshape(own_rows, width)).reshape(tokens, width)
    x_all = packed[:, :own_rows].reshape(tokens, width).astype(f32)
    g_bc, g_gain, g_cbc, g_bbc = unpack(packed[:, own_rows:].reshape(groups, -1), small_shapes)
    wbc = g_bc.reshape(width, maps)
    gain = g_gain.reshape(width).astype(f32)
    convbc = jnp.transpose(g_cbc, (1, 0, 2)).reshape(taps, maps)
    biasbc = g_bbc.reshape(maps)

    normed_low = pre_norm(x_all, gain).astype(low)
    wx, wz = w_xz[:, 0], w_xz[:, 1]
    w_conv = jnp.concatenate([wx, wbc], 1)
    conv_low = jnp.dot(normed_low, w_conv, preferred_element_type=f32).astype(low)
    conv_low = conv_low.reshape(seqs, rows, inner + maps)
    gate_in = jnp.dot(normed_low, wz, preferred_element_type=f32)
    dt_raw = jnp.dot(normed_low, w_dt, preferred_element_type=f32)
    previous = shifted(conv_low[:, rows - edge :], "ctx", 1)
    extended = jnp.concatenate([previous, conv_low], 1).astype(f32)
    conv_w = jnp.concatenate([conv_x, convbc], -1).astype(f32)
    conv_b = jnp.concatenate([conv_bias_x, biasbc], -1).astype(f32)
    conv_out, conv_back = jax.vjp(conv_silu, extended, conv_w, conv_b)
    mixed = conv_out.astype(low).astype(f32)
    x_heads = mixed[..., :inner].reshape(seqs, rows, heads, head_size)
    b_mat = mixed[..., inner : inner + state]
    c_mat = mixed[..., inner + state :]
    local_out, ssd_back = jax.vjp(
        ssd_local,
        x_heads,
        b_mat,
        c_mat,
        dt_raw.reshape(seqs, rows, heads),
        dt_bias.astype(f32),
        a_log.astype(f32),
        d_skip.astype(f32),
    )
    y_loc, growth, decay, s_loc = local_out
    identity = (jnp.ones_like(decay), jnp.zeros_like(s_loc))
    s_in = entering_2((decay, s_loc), "ctx", chain_step, identity)[1]
    y_off, read_back = jax.vjp(state_read, c_mat, growth, s_in)
    y_all = (y_loc + y_off).reshape(tokens, inner)
    sigma = jax.nn.sigmoid(gate_in)
    gate_act = gate_in * sigma
    gated = y_all * gate_act
    gain_gate = gate_gain.astype(f32)
    d_out = lax.dot_general(cot_low, w_out, (((1,), (1,)), ((), ())), preferred_element_type=f32)
    weighted = d_out * gain_gate
    stats = jnp.stack([jnp.sum(gated * gated, -1), jnp.sum(weighted * gated, -1)])
    stats = lax.psum(stats, ("fsdp", "tp"))
    scale = lax.rsqrt(stats[0] / inner_total + EPSILON)[:, None]
    inner_stat = stats[1][:, None] / inner_total
    branch = jnp.dot((gated * gain_gate).astype(low), w_out, preferred_element_type=f32)
    branch = scatter_sum(branch.astype(low).reshape(groups, own_rows, width)).astype(f32)
    scale_own = lax.dynamic_slice_in_dim(scale, own * own_rows, own_rows, 0)
    block_out = (x_own.astype(f32) + branch * scale_own).astype(low)

    normed_out = (gated * scale * gain_gate).astype(low)
    grad_wout = lax.dot_general(
        normed_out, cot_low, (((0,), (0,)), ((), ())), preferred_element_type=f32
    )
    grad_gate = jnp.sum(d_out * gated * scale, 0)
    d_gated = scale * weighted - gated * (scale * scale * scale * inner_stat)
    d_y = (d_gated * gate_act).reshape(seqs, rows, heads, head_size)
    d_gate_in = (d_gated * y_all * sigma * (1.0 + gate_in * (1.0 - sigma))).astype(low)
    grad_wz = lax.dot_general(
        normed_low, d_gate_in, (((0,), (0,)), ((), ())), preferred_element_type=f32
    )
    early = jnp.concatenate(
        [grad_wout.astype(low), grad_wz.astype(low).reshape(-1, width)], 0
    )
    early = lax.psum(early, "ctx").astype(f32)
    sum_wout = early[:inner]
    sum_wz = early[inner:].reshape(width, inner)

    dc_read, dgrowth_read, direct = read_back(d_y)
    carried = entering_3((decay, direct), "ctx", chain_step, identity)[1]
    d_decay = jnp.sum(carried * s_in, (2, 3))
    d_xheads, d_bmat, d_cmat, d_dtraw, grad_dtbias, grad_alog, grad_dskip = ssd_back(
        (d_y, dgrowth_read, d_decay, carried)
    )
    d_mixed = jnp.concatenate(
        [d_xheads.reshape(seqs, rows, inner), d_bmat, d_cmat + dc_read], -1
    )
    d_extended, grad_convw, grad_convb = conv_back(d_mixed)
    returned = shifted(d_extended[:, :edge], "ctx", -1)
    d_conv = d_extended[:, edge:]
    d_conv = jnp.concatenate(
        [d_conv[:, : rows - edge], d_conv[:, rows - edge :] + returned], 1
    )
    d_conv_low = d_conv.reshape(tokens, inner + maps).astype(low)
    d_dt_low = d_dtraw.reshape(tokens, heads).astype(low)
    nt = (((1,), (1,)), ((), ()))
    d_normed = lax.dot_general(d_conv_low, w_conv, nt, preferred_element_type=f32)
    d_normed = d_normed + lax.dot_general(d_gate_in, wz, nt, preferred_element_type=f32)
    d_normed = d_normed + lax.dot_general(d_dt_low, w_dt, nt, preferred_element_type=f32)
    grad_conv_all = lax.dot_general(
        normed_low, d_conv_low, (((0,), (0,)), ((), ())), preferred_element_type=f32
    )
    grad_wdt = lax.dot_general(
        normed_low, d_dt_low, (((0,), (0,)), ((), ())), preferred_element_type=f32
    )
    grad_wx, grad_wbc = grad_conv_all[:, :inner], grad_conv_all[:, inner:]

    tail = jnp.concatenate(
        [
            grad_wbc.astype(low).reshape(groups, -1),
            jnp.transpose(
                grad_convw[:, inner:].astype(low).reshape(taps, groups, -1), (1, 0, 2)
            ).reshape(groups, -1),
            grad_convb[inner:].astype(low).reshape(groups, -1),
        ],
        1,
    )
    tail_size = tail.shape[1]
    unit = width * 32
    tail = jnp.pad(tail, ((0, 0), (0, -(-tail_size // unit) * unit - tail_size)))
    tail = tail.reshape(groups, -1, width)
    sends = jnp.concatenate([d_normed.astype(low).reshape(groups, own_rows, width), tail], 1)
    got = scatter_sum(sends)
    d_normed_own = got[:own_rows].astype(f32)
    x_f = x_own.astype(f32)
    _, norm_back = jax.vjp(pre_norm, x_f, gain)
    d_inputs, grad_gain = norm_back(d_normed_own)
    input_grad = (out_cotangent.reshape(own_rows, width).astype(f32) + d_inputs).reshape(
        seq_own, rows, width
    )
    bc_part = got[own_rows:].reshape(-1)
    late_parts = (
        grad_wx,
        grad_wdt,
        grad_convw[:, :inner],
        grad_convb[:inner],
        grad_dtbias,
        grad_alog,
        grad_dskip,
        grad_gate,
    )
    late = pad_rows([part.astype(low) for part in late_parts], width, 32)
    late = lax.psum(late, "ctx").astype(f32)
    sum_wx, sum_wdt, sum_convx, sum_biasx, sum_dtbias, sum_alog, sum_dskip, sum_gate = unpack(
        late.reshape(-1), [part.shape for part in late_parts]
    )
    bc_sum = lax.psum(bc_part, "ctx").astype(f32)
    sum_wbc, sum_convbc, sum_biasbc = unpack(
        bc_sum, (w_bc.shape, conv_bc.shape, conv_bias_bc.shape)
    )
    gain_sum = lax.psum(grad_gain, ("fsdp", "ctx"))
    gain_own = norm_gain.shape[0]
    sum_gain = lax.dynamic_slice_in_dim(gain_sum, own * gain_own, gain_own, 0)
    return (
        block_out.reshape(seq_own, rows, width),
        input_grad,
        sum_gain,
        jnp.stack([sum_wx, sum_wz], 1),
        sum_wbc,
        sum_wdt,
        sum_convx,
        sum_convbc,
        sum_biasx,
        sum_biasbc,
        sum_dtbias,
        sum_alog,
        sum_dskip,
        sum_gate,
        sum_wout,
    )


def solution(mesh):
    in_specs = (
        P("fsdp", "ctx", None),
        P("fsdp"),
        P(None, None, ("fsdp", "tp")),
        P("fsdp", None),
        P(None, ("fsdp", "tp")),
        P(None, ("fsdp", "tp")),
        P(None, "fsdp"),
        P(("fsdp", "tp")),
        P("fsdp"),
        P(("fsdp", "tp")),
        P(("fsdp", "tp")),
        P(("fsdp", "tp")),
        P(("fsdp", "tp")),
        P(("fsdp", "tp"), None),
        P("fsdp", "ctx", None),
    )
    out_specs = (
        P("fsdp", "ctx", None),
        P("fsdp", "ctx", None),
        P("fsdp"),
        P(None, None, ("fsdp", "tp")),
        P("fsdp", None),
        P(None, ("fsdp", "tp")),
        P(None, ("fsdp", "tp")),
        P(None, "fsdp"),
        P(("fsdp", "tp")),
        P("fsdp"),
        P(("fsdp", "tp")),
        P(("fsdp", "tp")),
        P(("fsdp", "tp")),
        P(("fsdp", "tp")),
        P(("fsdp", "tp"), None),
    )
    return jax.shard_map(body, mesh=mesh, in_specs=in_specs, out_specs=out_specs, check_vma=False)
```

```python
import functools

import jax
import jax.numpy as jnp
from jax import lax
from jax.experimental import pallas as pl
from jax.experimental.pallas import tpu as pltpu
from jax.sharding import PartitionSpec as P

EPSILON = 1e-05
PRECISE = lax.Precision.DEFAULT


def shifted(value, axis, steps):
    count = lax.axis_size(axis)
    initial, last = (max(0, -steps), min(count, count - steps))
    return lax.ppermute(value, axis, [(source, source + steps) for source in range(initial, last)])


def entering_2(x, axis, combine, identity):
    count, place = (lax.axis_size(axis), lax.axis_index(axis))
    everything = jax.tree.map(
        lambda part, kind: lax.all_gather(part.astype(kind), axis), x, (jnp.bfloat16, jnp.bfloat16)
    )
    start = jax.tree.map(
        lambda part, zero: jnp.broadcast_to(jnp.asarray(zero, part.dtype), part.shape), x, identity
    )

    def hop(k, before):
        reached = k < place
        new = combine(
            before, jax.tree.map(lambda part, own: part[k].astype(own.dtype), everything, x)
        )
        return jax.tree.map(lambda a, b: jnp.where(reached, a, b), new, before)

    return lax.fori_loop(0, count, hop, start)


def entering_3(x, axis, join, neutral):
    count = lax.axis_size(axis)
    place = lax.axis_index(axis)
    ahead = count - 1 - place
    gathered = jax.tree.map(
        lambda a, kind: lax.all_gather(a.astype(kind), axis),
        x,
        jax.tree.map(lambda a: jnp.bfloat16 if a.dtype == jnp.float32 else a.dtype, x),
    )
    state = jax.tree.map(lambda a, e: jnp.zeros_like(a) + jnp.asarray(e, a.dtype), x, neutral)

    def one(hop, state):
        source = count - 1 - hop
        return join(
            state,
            jax.tree.map(
                lambda a, own: lax.dynamic_index_in_dim(a, source, 0, False).astype(own.dtype),
                gathered,
                x,
            ),
        )

    return lax.fori_loop(0, ahead, one, state)


def pre_norm(values, gain):
    mean_sq = jnp.mean(values * values, -1, keepdims=True)
    return values * lax.rsqrt(mean_sq + EPSILON) * gain


def conv_silu(extended, taps_w, taps_b):
    tap_count = taps_w.shape[0]
    out_rows = extended.shape[1] - tap_count + 1
    running = taps_b + extended[:, 0:out_rows] * taps_w[0]
    for offset in range(1, tap_count):
        running = running + extended[:, offset : offset + out_rows] * taps_w[offset]
    return jax.nn.silu(running)


def ssd_local(x_heads, b_mat, c_mat, dt_raw, dt_bias, a_log, d_skip):
    step_size = jax.nn.softplus(dt_raw + dt_bias)
    log_decay = -step_size * jnp.exp(a_log)
    upto = jnp.tril(jnp.ones((log_decay.shape[1],) * 2, jnp.float32))
    cumul = jnp.einsum("lm,smh->slh", upto, log_decay, precision=lax.Precision.HIGHEST)
    across = jnp.transpose(cumul, (0, 2, 1))
    step_t = jnp.transpose(step_size, (0, 2, 1))
    block_len = x_heads.shape[1]
    later_pos = lax.broadcasted_iota(jnp.int32, (block_len, block_len), 0)
    earlier_pos = lax.broadcasted_iota(jnp.int32, (block_len, block_len), 1)
    causal = later_pos >= earlier_pos
    gaps = across[:, :, :, None] - across[:, :, None, :]
    kernel = jnp.exp(jnp.where(causal, gaps, -1e30))
    scores = jnp.einsum("sln,smn->slm", c_mat, b_mat, precision=PRECISE)
    mixing = scores[:, None] * kernel * step_t[:, :, None, :]
    y_loc = (
        jnp.einsum("shlm,smhp->slhp", mixing, x_heads, precision=PRECISE)
        + d_skip[:, None] * x_heads
    )
    final = across[:, :, -1:]
    carry_w = jnp.exp(final - across) * step_t
    scaled = x_heads * jnp.transpose(carry_w, (0, 2, 1))[..., None]
    s_loc = jnp.einsum("slhp,sln->shpn", scaled, b_mat, precision=PRECISE)
    return (y_loc, jnp.exp(cumul), jnp.exp(final[..., 0]), s_loc)


def state_read(c_mat, growth, s_in):
    reading = jnp.einsum("sln,shpn->slhp", c_mat, s_in, precision=PRECISE)
    return growth[..., None] * reading


def chain_step(earlier, later):
    return (earlier[0] * later[0], earlier[1] * later[0][:, :, None, None] + later[1])


MESH = pl.DeviceIdType.MESH


def greet(peers):
    barrier = pltpu.get_barrier_semaphore()
    for peer in peers:
        pl.semaphore_signal(barrier, inc=1, device_id=peer, device_id_type=MESH)
    pl.semaphore_wait(barrier, len(peers))


def other(axis, steps):
    return {axis: lax.rem(lax.axis_index(axis) + steps, lax.axis_size(axis))}


def finish_kernel(
    groups,
    blocks,
    token_half,
    sends,
    late,
    scaled_x,
    out_d,
    out_late,
    out_tail,
    out_gain,
    pair_buf,
    pair_sum,
    row_buf,
    late_buf,
    acc,
    tail_own,
    tail_buf,
    gain_own,
    gain_buf,
    gain_rows,
    gain_row_buf,
    gain_pair,
    gain_pair_buf,
    pair_sems,
    row_sems,
    late_sems,
    spread_sems,
    tail_sems,
    gain_sems,
    gain_row_sems,
    last_sems,
):
    f32, low = jnp.float32, jnp.bfloat16
    own = lax.axis_index("fsdp")
    place = lax.axis_index("ctx")
    core = lax.axis_index("tp")
    partner = other("tp", 1)
    row_peers = [other("fsdp", k) for k in range(1, groups)]
    block_peers = [other("ctx", j) for j in range(1, blocks)]
    greet([partner] + row_peers + block_peers)

    def remote(source, target, sems, at, device):
        copy = pltpu.make_async_remote_copy(
            src_ref=source,
            dst_ref=target,
            send_sem=sems.at[0, at],
            recv_sem=sems.at[1, at],
            device_id=device,
            device_id_type=MESH,
        )
        copy.start()
        return copy

    order = list(range(1, groups)) + [0]
    pair = {}
    for k in order:
        row = lax.rem(own + k, groups)
        pair[k] = remote(sends.at[row, 1 - core], pair_buf.at[k], pair_sems, k, partner)
    lates = []
    for j in range(1, blocks):
        where = lax.rem(place + j, blocks)
        lates.append(remote(late.at[where], late_buf.at[j], late_sems, j, block_peers[j - 1]))
    rowc = []
    for k in order:
        row = lax.rem(own + k, groups)
        pair[k].wait_recv()
        total = sends[row, core].astype(f32) + pair_buf[k].astype(f32)
        if k:
            pair_sum[k] = total.astype(low)
            rowc.append(remote(pair_sum.at[k], row_buf.at[k], row_sems, k, row_peers[k - 1]))
        else:
            acc[...] = total
    part = late[place].astype(f32)
    for j in range(1, blocks):
        lates[j - 1].wait_recv()
        part = part + late_buf[j].astype(f32)
    out_late[place] = part.astype(low)
    spread = []
    for j in range(1, blocks):
        spread.append(
            remote(out_late.at[place], out_late.at[place], spread_sems, j, block_peers[j - 1])
        )
    for k in range(1, groups):
        rowc[k - 1].wait_recv()
        acc[...] += row_buf[k].astype(f32)
    tail_own[...] = acc[token_half:].astype(low)
    tails = [
        remote(tail_own, tail_buf.at[j], tail_sems, j, block_peers[j - 1])
        for j in range(1, blocks)
    ]
    out_d[core] = acc[:token_half].astype(low)
    d_copy = remote(out_d.at[core], out_d.at[core], last_sems, 0, partner)
    gain = jnp.sum(acc[:token_half] * scaled_x[core], 0, keepdims=True)
    gain_own[...] = jnp.broadcast_to(gain, gain_own.shape)
    gains = [
        remote(gain_own, gain_buf.at[j], gain_sems, j, block_peers[j - 1])
        for j in range(1, blocks)
    ]
    gain = gain_own[...]
    for j in range(1, blocks):
        gains[j - 1].wait_recv()
        gain = gain + gain_buf[j]
    gain_rows[...] = gain
    gain_sent = [
        remote(gain_rows, gain_row_buf.at[k], gain_row_sems, k, row_peers[k - 1])
        for k in range(1, groups)
    ]
    tail = tail_own[...].astype(f32)
    for j in range(1, blocks):
        tails[j - 1].wait_recv()
        tail = tail + tail_buf[j].astype(f32)
    out_tail[core] = tail.astype(low)
    tail_copy = remote(out_tail.at[core], out_tail.at[core], last_sems, 1, partner)
    gain = gain_rows[...]
    for k in range(1, groups):
        gain_sent[k - 1].wait_recv()
        gain = gain + gain_row_buf[k]
    gain_pair[...] = gain
    gain_copy = remote(gain_pair, gain_pair_buf, last_sems, 2, partner)
    for copy in spread:
        copy.wait_recv()
    d_copy.wait_recv()
    tail_copy.wait_recv()
    gain_copy.wait_recv()
    out_gain[...] = gain_pair[...] + gain_pair_buf[...]
    everything = list(pair.values()) + lates + rowc + spread + tails + gains + gain_sent
    for copy in everything + [d_copy, tail_copy, gain_copy]:
        copy.wait_send()


def finish(sends, late, scaled_x, token_half):
    groups, _, half, width = sends.shape
    blocks, quota, _ = late.shape
    tail_half = half - token_half
    f32, low = jnp.float32, jnp.bfloat16
    vmem = pl.BlockSpec(memory_space=pltpu.VMEM)
    dma = pltpu.SemaphoreType.DMA
    return pl.pallas_call(
        functools.partial(finish_kernel, groups, blocks, token_half),
        out_shape=(
            jax.ShapeDtypeStruct((2, token_half, width), low),
            jax.ShapeDtypeStruct((blocks, quota, width), low),
            jax.ShapeDtypeStruct((2, tail_half, width), low),
            jax.ShapeDtypeStruct((8, width), f32),
        ),
        in_specs=[vmem] * 3,
        out_specs=(vmem,) * 4,
        scratch_shapes=[
            pltpu.VMEM((groups, half, width), low),
            pltpu.VMEM((groups, half, width), low),
            pltpu.VMEM((groups, half, width), low),
            pltpu.VMEM((blocks, quota, width), low),
            pltpu.VMEM((half, width), f32),
            pltpu.VMEM((tail_half, width), low),
            pltpu.VMEM((blocks, tail_half, width), low),
            pltpu.VMEM((8, width), f32),
            pltpu.VMEM((blocks, 8, width), f32),
            pltpu.VMEM((8, width), f32),
            pltpu.VMEM((groups, 8, width), f32),
            pltpu.VMEM((8, width), f32),
            pltpu.VMEM((8, width), f32),
            dma((2, groups)),
            dma((2, groups)),
            dma((2, blocks)),
            dma((2, blocks)),
            dma((2, blocks)),
            dma((2, blocks)),
            dma((2, groups)),
            dma((2, 3)),
        ],
        compiler_params=pltpu.CompilerParams(
            collective_id=0, has_side_effects=True, vmem_limit_bytes=48 * 1024 * 1024
        ),
        cost_estimate=pl.CostEstimate(flops=10**7, bytes_accessed=10**8, transcendentals=0),
        name="finish",
    )(sends, late, scaled_x)


def pad_rows(parts, width, multiple):
    flat = jnp.concatenate([part.reshape(-1) for part in parts])
    unit = width * multiple
    total = -(-flat.shape[0] // unit) * unit
    return jnp.pad(flat, (0, total - flat.shape[0])).reshape(-1, width)


def unpack(flat, shapes):
    out, at = [], 0
    for shape in shapes:
        size = 1
        for n in shape:
            size *= n
        out.append(flat[..., at : at + size].reshape(flat.shape[:-1] + tuple(shape)))
        at += size
    return out


def gather_rows(x):
    half = x.shape[0] // lax.axis_size("tp")
    mine = lax.dynamic_slice_in_dim(x, lax.axis_index("tp") * half, half, 0)
    full = lax.all_gather(mine, ("fsdp", "tp"))
    return full.reshape((lax.axis_size("fsdp"),) + x.shape)


def scatter_sum(x):
    part = lax.psum_scatter(x, "fsdp", scatter_dimension=0, tiled=False)
    return lax.psum(part, "tp")


def body(
    block_input,
    norm_gain,
    w_xz,
    w_bc,
    w_dt,
    conv_x,
    conv_bc,
    conv_bias_x,
    conv_bias_bc,
    dt_bias,
    a_log,
    d_skip,
    gate_gain,
    w_out,
    out_cotangent,
):
    f32, low = jnp.float32, jnp.bfloat16
    groups = lax.axis_size("fsdp")
    own = lax.axis_index("fsdp")
    seq_own, rows, width = block_input.shape
    own_rows = seq_own * rows
    seqs = groups * seq_own
    tokens = seqs * rows
    inner = w_xz.shape[2]
    inner_total = inner * groups * lax.axis_size("tp")
    maps = w_bc.shape[1]
    state = maps // 2
    heads = w_dt.shape[1]
    head_size = inner // heads
    taps = conv_x.shape[0]
    edge = taps - 1

    small_shapes = (w_bc.shape, norm_gain.shape, conv_bc.shape, conv_bias_bc.shape)
    small = pad_rows((w_bc, norm_gain, conv_bc, conv_bias_bc), width, 32)
    x_own = block_input.reshape(own_rows, width)
    packed = gather_rows(jnp.concatenate([x_own, small], 0))
    cot_low = gather_rows(out_cotangent.reshape(own_rows, width)).reshape(tokens, width)
    x_all = packed[:, :own_rows].reshape(tokens, width).astype(f32)
    g_bc, g_gain, g_cbc, g_bbc = unpack(packed[:, own_rows:].reshape(groups, -1), small_shapes)
    wbc = g_bc.reshape(width, maps)
    gain = g_gain.reshape(width).astype(f32)
    convbc = jnp.transpose(g_cbc, (1, 0, 2)).reshape(taps, maps)
    biasbc = g_bbc.reshape(maps)

    normed_low = pre_norm(x_all, gain).astype(low)
    wx, wz = w_xz[:, 0], w_xz[:, 1]
    w_conv = jnp.concatenate([wx, wbc], 1)
    conv_low = jnp.dot(normed_low, w_conv, preferred_element_type=f32).astype(low)
    conv_low = conv_low.reshape(seqs, rows, inner + maps)
    gate_in = jnp.dot(normed_low, wz, preferred_element_type=f32)
    dt_raw = jnp.dot(normed_low, w_dt, preferred_element_type=f32)
    previous = shifted(conv_low[:, rows - edge :], "ctx", 1)
    extended = jnp.concatenate([previous, conv_low], 1).astype(f32)
    conv_w = jnp.concatenate([conv_x, convbc], -1).astype(f32)
    conv_b = jnp.concatenate([conv_bias_x, biasbc], -1).astype(f32)
    conv_out, conv_back = jax.vjp(conv_silu, extended, conv_w, conv_b)
    mixed = conv_out.astype(low).astype(f32)
    x_heads = mixed[..., :inner].reshape(seqs, rows, heads, head_size)
    b_mat = mixed[..., inner : inner + state]
    c_mat = mixed[..., inner + state :]
    local_out, ssd_back = jax.vjp(
        ssd_local,
        x_heads,
        b_mat,
        c_mat,
        dt_raw.reshape(seqs, rows, heads),
        dt_bias.astype(f32),
        a_log.astype(f32),
        d_skip.astype(f32),
    )
    y_loc, growth, decay, s_loc = local_out
    identity = (jnp.ones_like(decay), jnp.zeros_like(s_loc))
    s_in = entering_2((decay, s_loc), "ctx", chain_step, identity)[1]
    y_off, read_back = jax.vjp(state_read, c_mat, growth, s_in)
    y_all = (y_loc + y_off).reshape(tokens, inner)
    sigma = jax.nn.sigmoid(gate_in)
    gate_act = gate_in * sigma
    gated = y_all * gate_act
    gain_gate = gate_gain.astype(f32)
    d_out = lax.dot_general(cot_low, w_out, (((1,), (1,)), ((), ())), preferred_element_type=f32)
    weighted = d_out * gain_gate
    stats = jnp.stack([jnp.sum(gated * gated, -1), jnp.sum(weighted * gated, -1)])
    stats = lax.psum(stats, ("fsdp", "tp"))
    scale = lax.rsqrt(stats[0] / inner_total + EPSILON)[:, None]
    inner_stat = stats[1][:, None] / inner_total
    branch = jnp.dot((gated * gain_gate).astype(low), w_out, preferred_element_type=f32)
    branch = scatter_sum(branch.astype(low).reshape(groups, own_rows, width)).astype(f32)
    scale_own = lax.dynamic_slice_in_dim(scale, own * own_rows, own_rows, 0)
    block_out = (x_own.astype(f32) + branch * scale_own).astype(low)

    normed_out = (gated * scale * gain_gate).astype(low)
    grad_wout = lax.dot_general(
        normed_out, cot_low, (((0,), (0,)), ((), ())), preferred_element_type=f32
    )
    grad_gate = jnp.sum(d_out * gated * scale, 0)
    d_gated = scale * weighted - gated * (scale * scale * scale * inner_stat)
    d_y = (d_gated * gate_act).reshape(seqs, rows, heads, head_size)
    d_gate_in = (d_gated * y_all * sigma * (1.0 + gate_in * (1.0 - sigma))).astype(low)
    grad_wz = lax.dot_general(
        normed_low, d_gate_in, (((0,), (0,)), ((), ())), preferred_element_type=f32
    )
    early = jnp.concatenate(
        [grad_wout.astype(low), grad_wz.astype(low).reshape(-1, width)], 0
    )
    early = lax.psum(early, "ctx").astype(f32)
    sum_wout = early[:inner]
    sum_wz = early[inner:].reshape(width, inner)

    dc_read, dgrowth_read, direct = read_back(d_y)
    carried = entering_3((decay, direct), "ctx", chain_step, identity)[1]
    d_decay = jnp.sum(carried * s_in, (2, 3))
    d_xheads, d_bmat, d_cmat, d_dtraw, grad_dtbias, grad_alog, grad_dskip = ssd_back(
        (d_y, dgrowth_read, d_decay, carried)
    )
    d_mixed = jnp.concatenate(
        [d_xheads.reshape(seqs, rows, inner), d_bmat, d_cmat + dc_read], -1
    )
    d_extended, grad_convw, grad_convb = conv_back(d_mixed)
    returned = shifted(d_extended[:, :edge], "ctx", -1)
    d_conv = d_extended[:, edge:]
    d_conv = jnp.concatenate(
        [d_conv[:, : rows - edge], d_conv[:, rows - edge :] + returned], 1
    )
    d_conv_low = d_conv.reshape(tokens, inner + maps).astype(low)
    d_dt_low = d_dtraw.reshape(tokens, heads).astype(low)
    nt = (((1,), (1,)), ((), ()))
    d_normed = lax.dot_general(d_conv_low, w_conv, nt, preferred_element_type=f32)
    d_normed = d_normed + lax.dot_general(d_gate_in, wz, nt, preferred_element_type=f32)
    d_normed = d_normed + lax.dot_general(d_dt_low, w_dt, nt, preferred_element_type=f32)
    grad_conv_all = lax.dot_general(
        normed_low, d_conv_low, (((0,), (0,)), ((), ())), preferred_element_type=f32
    )
    grad_wdt = lax.dot_general(
        normed_low, d_dt_low, (((0,), (0,)), ((), ())), preferred_element_type=f32
    )
    grad_wx, grad_wbc = grad_conv_all[:, :inner], grad_conv_all[:, inner:]

    tail = jnp.concatenate(
        [
            grad_wbc.astype(low).reshape(groups, -1),
            jnp.transpose(
                grad_convw[:, inner:].astype(low).reshape(taps, groups, -1), (1, 0, 2)
            ).reshape(groups, -1),
            grad_convb[inner:].astype(low).reshape(groups, -1),
        ],
        1,
    )
    tail_size = tail.shape[1]
    unit = width * 32
    tail = jnp.pad(tail, ((0, 0), (0, -(-tail_size // unit) * unit - tail_size)))
    token_half = own_rows // 2
    sends = jnp.concatenate(
        [
            d_normed.astype(low).reshape(groups, 2, token_half, width),
            tail.reshape(groups, 2, -1, width),
        ],
        2,
    )
    late_parts = (
        grad_wx,
        grad_wdt,
        grad_convw[:, :inner],
        grad_convb[:inner],
        grad_dtbias,
        grad_alog,
        grad_dskip,
        grad_gate,
    )
    blocks = lax.axis_size("ctx")
    late = pad_rows([part.astype(low) for part in late_parts], width, 16 * blocks)
    x_f = x_own.astype(f32)
    r1 = lax.rsqrt(jnp.mean(x_f * x_f, -1, keepdims=True) + EPSILON)
    scaled_x = (x_f * r1).reshape(2, token_half, width)
    got_d, late, bc_sum, gain_sum = finish(
        sends, late.reshape(blocks, -1, width), scaled_x, token_half
    )
    d_normed_own = got_d.reshape(own_rows, width).astype(f32)
    b = d_normed_own * gain
    d_inputs = r1 * b - x_f * (r1 * r1 * r1) * jnp.mean(b * x_f, -1, keepdims=True)
    input_grad = (out_cotangent.reshape(own_rows, width).astype(f32) + d_inputs).reshape(
        seq_own, rows, width
    )
    late = late.astype(f32)
    bc_sum = bc_sum.reshape(-1).astype(f32)
    sum_wx, sum_wdt, sum_convx, sum_biasx, sum_dtbias, sum_alog, sum_dskip, sum_gate = unpack(
        late.reshape(-1), [part.shape for part in late_parts]
    )
    sum_wbc, sum_convbc, sum_biasbc = unpack(
        bc_sum, (w_bc.shape, conv_bc.shape, conv_bias_bc.shape)
    )
    gain_own = norm_gain.shape[0]
    sum_gain = lax.dynamic_slice_in_dim(gain_sum[0], own * gain_own, gain_own, 0)
    return (
        block_out.reshape(seq_own, rows, width),
        input_grad,
        sum_gain,
        jnp.stack([sum_wx, sum_wz], 1),
        sum_wbc,
        sum_wdt,
        sum_convx,
        sum_convbc,
        sum_biasx,
        sum_biasbc,
        sum_dtbias,
        sum_alog,
        sum_dskip,
        sum_gate,
        sum_wout,
    )


def solution(mesh):
    in_specs = (
        P("fsdp", "ctx", None),
        P("fsdp"),
        P(None, None, ("fsdp", "tp")),
        P("fsdp", None),
        P(None, ("fsdp", "tp")),
        P(None, ("fsdp", "tp")),
        P(None, "fsdp"),
        P(("fsdp", "tp")),
        P("fsdp"),
        P(("fsdp", "tp")),
        P(("fsdp", "tp")),
        P(("fsdp", "tp")),
        P(("fsdp", "tp")),
        P(("fsdp", "tp"), None),
        P("fsdp", "ctx", None),
    )
    out_specs = (
        P("fsdp", "ctx", None),
        P("fsdp", "ctx", None),
        P("fsdp"),
        P(None, None, ("fsdp", "tp")),
        P("fsdp", None),
        P(None, ("fsdp", "tp")),
        P(None, ("fsdp", "tp")),
        P(None, "fsdp"),
        P(("fsdp", "tp")),
        P("fsdp"),
        P(("fsdp", "tp")),
        P(("fsdp", "tp")),
        P(("fsdp", "tp")),
        P(("fsdp", "tp")),
        P(("fsdp", "tp"), None),
    )
    return jax.shard_map(body, mesh=mesh, in_specs=in_specs, out_specs=out_specs, check_vma=False)
```

```python
import functools

import jax
import jax.numpy as jnp
from jax import lax
from jax.experimental import pallas as pl
from jax.experimental.pallas import tpu as pltpu
from jax.sharding import PartitionSpec as P

EPSILON = 1e-05
PRECISE = lax.Precision.DEFAULT


def shifted(value, axis, steps):
    count = lax.axis_size(axis)
    initial, last = (max(0, -steps), min(count, count - steps))
    return lax.ppermute(value, axis, [(source, source + steps) for source in range(initial, last)])


def pre_norm(values, gain):
    mean_sq = jnp.mean(values * values, -1, keepdims=True)
    return values * lax.rsqrt(mean_sq + EPSILON) * gain


def conv_silu(extended, taps_w, taps_b):
    tap_count = taps_w.shape[0]
    out_rows = extended.shape[1] - tap_count + 1
    running = taps_b + extended[:, 0:out_rows] * taps_w[0]
    for offset in range(1, tap_count):
        running = running + extended[:, offset : offset + out_rows] * taps_w[offset]
    return jax.nn.silu(running)


def ssd_local(x_heads, b_mat, c_mat, dt_raw, dt_bias, a_log, d_skip):
    step_size = jax.nn.softplus(dt_raw + dt_bias)
    log_decay = -step_size * jnp.exp(a_log)
    upto = jnp.tril(jnp.ones((log_decay.shape[1],) * 2, jnp.float32))
    cumul = jnp.einsum("lm,smh->slh", upto, log_decay, precision=lax.Precision.HIGHEST)
    across = jnp.transpose(cumul, (0, 2, 1))
    step_t = jnp.transpose(step_size, (0, 2, 1))
    block_len = x_heads.shape[1]
    later_pos = lax.broadcasted_iota(jnp.int32, (block_len, block_len), 0)
    earlier_pos = lax.broadcasted_iota(jnp.int32, (block_len, block_len), 1)
    causal = later_pos >= earlier_pos
    gaps = across[:, :, :, None] - across[:, :, None, :]
    kernel = jnp.exp(jnp.where(causal, gaps, -1e30))
    scores = jnp.einsum("sln,smn->slm", c_mat, b_mat, precision=PRECISE)
    mixing = scores[:, None] * kernel * step_t[:, :, None, :]
    y_loc = (
        jnp.einsum("shlm,smhp->slhp", mixing, x_heads, precision=PRECISE)
        + d_skip[:, None] * x_heads
    )
    final = across[:, :, -1:]
    carry_w = jnp.exp(final - across) * step_t
    scaled = x_heads * jnp.transpose(carry_w, (0, 2, 1))[..., None]
    s_loc = jnp.einsum("slhp,sln->shpn", scaled, b_mat, precision=PRECISE)
    return (y_loc, jnp.exp(cumul), jnp.exp(final[..., 0]), s_loc)


def state_read(c_mat, growth, s_in):
    reading = jnp.einsum("sln,shpn->slhp", c_mat, s_in, precision=PRECISE)
    return growth[..., None] * reading


MESH = pl.DeviceIdType.MESH


def greet(peers):
    barrier = pltpu.get_barrier_semaphore()
    for peer in peers:
        pl.semaphore_signal(barrier, inc=1, device_id=peer, device_id_type=MESH)
    pl.semaphore_wait(barrier, len(peers))


def other(axis, steps):
    return {axis: lax.rem(lax.axis_index(axis) + steps, lax.axis_size(axis))}


def finish_kernel(
    groups,
    blocks,
    token_half,
    sends,
    late,
    scaled_x,
    out_d,
    out_late,
    out_tail,
    out_gain,
    pair_buf,
    pair_sum,
    row_buf,
    late_buf,
    acc,
    tail_own,
    tail_buf,
    gain_own,
    gain_buf,
    gain_rows,
    gain_row_buf,
    gain_pair,
    gain_pair_buf,
    pair_sems,
    row_sems,
    late_sems,
    spread_sems,
    tail_sems,
    gain_sems,
    gain_row_sems,
    last_sems,
):
    f32, low = jnp.float32, jnp.bfloat16
    own = lax.axis_index("fsdp")
    place = lax.axis_index("ctx")
    core = lax.axis_index("tp")
    partner = other("tp", 1)
    row_peers = [other("fsdp", k) for k in range(1, groups)]
    block_peers = [other("ctx", j) for j in range(1, blocks)]
    greet([partner] + row_peers + block_peers)

    def remote(source, target, sems, at, device):
        copy = pltpu.make_async_remote_copy(
            src_ref=source,
            dst_ref=target,
            send_sem=sems.at[0, at],
            recv_sem=sems.at[1, at],
            device_id=device,
            device_id_type=MESH,
        )
        copy.start()
        return copy

    order = list(range(1, groups)) + [0]
    pair = {}
    for k in order:
        row = lax.rem(own + k, groups)
        pair[k] = remote(sends.at[row, 1 - core], pair_buf.at[k], pair_sems, k, partner)
    lates = []
    for j in range(1, blocks):
        where = lax.rem(place + j, blocks)
        lates.append(remote(late.at[where], late_buf.at[j], late_sems, j, block_peers[j - 1]))
    rowc = []
    for k in order:
        row = lax.rem(own + k, groups)
        pair[k].wait_recv()
        total = sends[row, core].astype(f32) + pair_buf[k].astype(f32)
        if k:
            pair_sum[k] = total.astype(low)
            rowc.append(remote(pair_sum.at[k], row_buf.at[k], row_sems, k, row_peers[k - 1]))
        else:
            acc[...] = total
    part = late[place].astype(f32)
    for j in range(1, blocks):
        lates[j - 1].wait_recv()
        part = part + late_buf[j].astype(f32)
    out_late[place] = part.astype(low)
    spread = []
    for j in range(1, blocks):
        spread.append(
            remote(out_late.at[place], out_late.at[place], spread_sems, j, block_peers[j - 1])
        )
    for k in range(1, groups):
        rowc[k - 1].wait_recv()
        acc[...] += row_buf[k].astype(f32)
    tail_own[...] = acc[token_half:].astype(low)
    tails = [
        remote(tail_own, tail_buf.at[j], tail_sems, j, block_peers[j - 1])
        for j in range(1, blocks)
    ]
    out_d[core] = acc[:token_half].astype(low)
    d_copy = remote(out_d.at[core], out_d.at[core], last_sems, 0, partner)
    gain = jnp.sum(acc[:token_half] * scaled_x[core], 0, keepdims=True)
    gain_own[...] = jnp.broadcast_to(gain, gain_own.shape)
    gains = [
        remote(gain_own, gain_buf.at[j], gain_sems, j, block_peers[j - 1])
        for j in range(1, blocks)
    ]
    gain = gain_own[...]
    for j in range(1, blocks):
        gains[j - 1].wait_recv()
        gain = gain + gain_buf[j]
    gain_rows[...] = gain
    gain_sent = [
        remote(gain_rows, gain_row_buf.at[k], gain_row_sems, k, row_peers[k - 1])
        for k in range(1, groups)
    ]
    tail = tail_own[...].astype(f32)
    for j in range(1, blocks):
        tails[j - 1].wait_recv()
        tail = tail + tail_buf[j].astype(f32)
    out_tail[core] = tail.astype(low)
    tail_copy = remote(out_tail.at[core], out_tail.at[core], last_sems, 1, partner)
    gain = gain_rows[...]
    for k in range(1, groups):
        gain_sent[k - 1].wait_recv()
        gain = gain + gain_row_buf[k]
    gain_pair[...] = gain
    gain_copy = remote(gain_pair, gain_pair_buf, last_sems, 2, partner)
    for copy in spread:
        copy.wait_recv()
    d_copy.wait_recv()
    tail_copy.wait_recv()
    gain_copy.wait_recv()
    out_gain[...] = gain_pair[...] + gain_pair_buf[...]
    everything = list(pair.values()) + lates + rowc + spread + tails + gains + gain_sent
    for copy in everything + [d_copy, tail_copy, gain_copy]:
        copy.wait_send()


def finish(sends, late, scaled_x, token_half):
    groups, _, half, width = sends.shape
    blocks = late.shape[0]
    tail_half = half - token_half
    f32, low = jnp.float32, jnp.bfloat16
    vmem = pl.BlockSpec(memory_space=pltpu.VMEM)
    dma = pltpu.SemaphoreType.DMA
    return pl.pallas_call(
        functools.partial(finish_kernel, groups, blocks, token_half),
        out_shape=(
            jax.ShapeDtypeStruct((2, token_half, width), low),
            jax.ShapeDtypeStruct(late.shape, low),
            jax.ShapeDtypeStruct((2, tail_half, width), low),
            jax.ShapeDtypeStruct((8, width), f32),
        ),
        in_specs=[vmem] * 3,
        out_specs=(vmem,) * 4,
        scratch_shapes=[
            pltpu.VMEM((groups, half, width), low),
            pltpu.VMEM((groups, half, width), low),
            pltpu.VMEM((groups, half, width), low),
            pltpu.VMEM(late.shape, low),
            pltpu.VMEM((half, width), f32),
            pltpu.VMEM((tail_half, width), low),
            pltpu.VMEM((blocks, tail_half, width), low),
            pltpu.VMEM((8, width), f32),
            pltpu.VMEM((blocks, 8, width), f32),
            pltpu.VMEM((8, width), f32),
            pltpu.VMEM((groups, 8, width), f32),
            pltpu.VMEM((8, width), f32),
            pltpu.VMEM((8, width), f32),
            dma((2, groups)),
            dma((2, groups)),
            dma((2, blocks)),
            dma((2, blocks)),
            dma((2, blocks)),
            dma((2, blocks)),
            dma((2, groups)),
            dma((2, 3)),
        ],
        compiler_params=pltpu.CompilerParams(
            collective_id=0, has_side_effects=True, vmem_limit_bytes=48 * 1024 * 1024
        ),
        cost_estimate=pl.CostEstimate(flops=10**7, bytes_accessed=10**8, transcendentals=0),
        name="finish",
    )(sends, late, scaled_x)


def carry_kernel(
    blocks, forward, state, decay, out, state_buf, decay_buf, state_sems, decay_sems
):
    place = lax.axis_index("ctx")
    greet([other("ctx", j) for j in range(1, blocks)])
    hops = []
    for j in range(1, blocks):
        ahead, behind = place + j < blocks, place >= j
        sending, receiving = (ahead, behind) if forward else (behind, ahead)
        pair = [
            pltpu.make_async_remote_copy(
                src_ref=source,
                dst_ref=target.at[j],
                send_sem=sems.at[0, j],
                recv_sem=sems.at[1, j],
                device_id=other("ctx", j if forward else blocks - j),
                device_id_type=MESH,
            )
            for source, target, sems in (
                (state, state_buf, state_sems),
                (decay, decay_buf, decay_sems),
            )
        ]

        @pl.when(sending)
        def _():
            pair[0].start()
            pair[1].start()

        hops.append((j, pair, sending, receiving))
    out[...] = jnp.zeros_like(out)
    for j, pair, sending, receiving in hops[::-1]:

        @pl.when(receiving)
        def _():
            pair[0].wait_recv()
            pair[1].wait_recv()
            out[...] = decay_buf[j][:, None, :] * out[...] + state_buf[j].astype(jnp.float32)

    for j, pair, sending, receiving in hops:

        @pl.when(sending)
        def _():
            pair[0].wait_send()
            pair[1].wait_send()


def carry(decay, state, forward):
    seqs, heads, size, depth = state.shape
    blocks = lax.axis_size("ctx")
    pairs = seqs * heads
    low, f32 = jnp.bfloat16, jnp.float32
    vmem = pl.BlockSpec(memory_space=pltpu.VMEM)
    wide = jnp.broadcast_to(decay.reshape(pairs, 1), (pairs, depth))
    out = pl.pallas_call(
        functools.partial(carry_kernel, blocks, forward),
        out_shape=jax.ShapeDtypeStruct((pairs, size, depth), f32),
        in_specs=[vmem] * 2,
        out_specs=vmem,
        scratch_shapes=[
            pltpu.VMEM((blocks, pairs, size, depth), low),
            pltpu.VMEM((blocks, pairs, depth), f32),
            pltpu.SemaphoreType.DMA((2, blocks)),
            pltpu.SemaphoreType.DMA((2, blocks)),
        ],
        compiler_params=pltpu.CompilerParams(
            collective_id=1 if forward else 2,
            has_side_effects=True,
            vmem_limit_bytes=32 * 1024 * 1024,
        ),
        name="states" if forward else "state_grads",
    )(state.reshape(pairs, size, depth).astype(low), wide)
    return out.reshape(state.shape)


def stats_kernel(groups, cores, part, out, buf, sems):
    where = [
        (k, t) for k in range(groups) for t in range(cores) if k + t > 0
    ]
    peers = [{**other("fsdp", k), **other("tp", t)} for k, t in where]
    greet(peers)
    copies = []
    for at, peer in enumerate(peers):
        copy = pltpu.make_async_remote_copy(
            src_ref=part,
            dst_ref=buf.at[at],
            send_sem=sems.at[0, at],
            recv_sem=sems.at[1, at],
            device_id=peer,
            device_id_type=MESH,
        )
        copy.start()
        copies.append(copy)
    total = part[...]
    for at, copy in enumerate(copies):
        copy.wait_recv()
        total = total + buf[at]
    out[...] = total
    for copy in copies:
        copy.wait_send()


def stats_sum(part):
    groups, cores = lax.axis_size("fsdp"), lax.axis_size("tp")
    flat = part.reshape(-1, 128)
    vmem = pl.BlockSpec(memory_space=pltpu.VMEM)
    peers = groups * cores - 1
    out = pl.pallas_call(
        functools.partial(stats_kernel, groups, cores),
        out_shape=jax.ShapeDtypeStruct(flat.shape, flat.dtype),
        in_specs=[vmem],
        out_specs=vmem,
        scratch_shapes=[
            pltpu.VMEM((peers,) + flat.shape, flat.dtype),
            pltpu.SemaphoreType.DMA((2, peers)),
        ],
        compiler_params=pltpu.CompilerParams(collective_id=3, has_side_effects=True),
        name="token_stats",
    )(flat)
    return out.reshape(part.shape)


def pad_rows(parts, width, multiple):
    flat = jnp.concatenate([part.reshape(-1) for part in parts])
    unit = width * multiple
    total = -(-flat.shape[0] // unit) * unit
    return jnp.pad(flat, (0, total - flat.shape[0])).reshape(-1, width)


def unpack(flat, shapes):
    out, at = [], 0
    for shape in shapes:
        size = 1
        for n in shape:
            size *= n
        out.append(flat[..., at : at + size].reshape(flat.shape[:-1] + tuple(shape)))
        at += size
    return out


def gather_rows(x):
    half = x.shape[0] // lax.axis_size("tp")
    mine = lax.dynamic_slice_in_dim(x, lax.axis_index("tp") * half, half, 0)
    full = lax.all_gather(mine, ("fsdp", "tp"))
    return full.reshape((lax.axis_size("fsdp"),) + x.shape)


def scatter_sum(x):
    part = lax.psum_scatter(x, "fsdp", scatter_dimension=0, tiled=False)
    return lax.psum(part, "tp")


def body(
    block_input,
    norm_gain,
    w_xz,
    w_bc,
    w_dt,
    conv_x,
    conv_bc,
    conv_bias_x,
    conv_bias_bc,
    dt_bias,
    a_log,
    d_skip,
    gate_gain,
    w_out,
    out_cotangent,
):
    f32, low = jnp.float32, jnp.bfloat16
    groups = lax.axis_size("fsdp")
    own = lax.axis_index("fsdp")
    seq_own, rows, width = block_input.shape
    own_rows = seq_own * rows
    seqs = groups * seq_own
    tokens = seqs * rows
    inner = w_xz.shape[2]
    inner_total = inner * groups * lax.axis_size("tp")
    maps = w_bc.shape[1]
    state = maps // 2
    heads = w_dt.shape[1]
    head_size = inner // heads
    taps = conv_x.shape[0]
    edge = taps - 1

    small_shapes = (w_bc.shape, norm_gain.shape, conv_bc.shape, conv_bias_bc.shape)
    small = pad_rows((w_bc, norm_gain, conv_bc, conv_bias_bc), width, 32)
    x_own = block_input.reshape(own_rows, width)
    packed = gather_rows(jnp.concatenate([x_own, small], 0))
    cot_low = gather_rows(out_cotangent.reshape(own_rows, width)).reshape(tokens, width)
    x_all = packed[:, :own_rows].reshape(tokens, width).astype(f32)
    g_bc, g_gain, g_cbc, g_bbc = unpack(packed[:, own_rows:].reshape(groups, -1), small_shapes)
    wbc = g_bc.reshape(width, maps)
    gain = g_gain.reshape(width).astype(f32)
    convbc = jnp.transpose(g_cbc, (1, 0, 2)).reshape(taps, maps)
    biasbc = g_bbc.reshape(maps)

    normed_low = pre_norm(x_all, gain).astype(low)
    wx, wz = w_xz[:, 0], w_xz[:, 1]
    w_conv = jnp.concatenate([wx, wbc], 1)
    conv_low = jnp.dot(normed_low, w_conv, preferred_element_type=f32).astype(low)
    conv_low = conv_low.reshape(seqs, rows, inner + maps)
    gate_in = jnp.dot(normed_low, wz, preferred_element_type=f32)
    dt_raw = jnp.dot(normed_low, w_dt, preferred_element_type=f32)
    previous = shifted(conv_low[:, rows - edge :], "ctx", 1)
    extended = jnp.concatenate([previous, conv_low], 1).astype(f32)
    conv_w = jnp.concatenate([conv_x, convbc], -1).astype(f32)
    conv_b = jnp.concatenate([conv_bias_x, biasbc], -1).astype(f32)
    conv_out, conv_back = jax.vjp(conv_silu, extended, conv_w, conv_b)
    mixed = conv_out.astype(low).astype(f32)
    x_heads = mixed[..., :inner].reshape(seqs, rows, heads, head_size)
    b_mat = mixed[..., inner : inner + state]
    c_mat = mixed[..., inner + state :]
    local_out, ssd_back = jax.vjp(
        ssd_local,
        x_heads,
        b_mat,
        c_mat,
        dt_raw.reshape(seqs, rows, heads),
        dt_bias.astype(f32),
        a_log.astype(f32),
        d_skip.astype(f32),
    )
    y_loc, growth, decay, s_loc = local_out
    s_in = carry(decay, s_loc, True)
    y_off, read_back = jax.vjp(state_read, c_mat, growth, s_in)
    y_all = (y_loc + y_off).reshape(tokens, inner)
    sigma = jax.nn.sigmoid(gate_in)
    gate_act = gate_in * sigma
    gated = y_all * gate_act
    gain_gate = gate_gain.astype(f32)
    d_out = lax.dot_general(cot_low, w_out, (((1,), (1,)), ((), ())), preferred_element_type=f32)
    weighted = d_out * gain_gate
    stats = jnp.stack([jnp.sum(gated * gated, -1), jnp.sum(weighted * gated, -1)])
    stats = stats_sum(stats)
    scale = lax.rsqrt(stats[0] / inner_total + EPSILON)[:, None]
    inner_stat = stats[1][:, None] / inner_total
    branch = jnp.dot((gated * gain_gate).astype(low), w_out, preferred_element_type=f32)
    branch = scatter_sum(branch.astype(low).reshape(groups, own_rows, width)).astype(f32)
    scale_own = lax.dynamic_slice_in_dim(scale, own * own_rows, own_rows, 0)
    block_out = (x_own.astype(f32) + branch * scale_own).astype(low)

    normed_out = (gated * scale * gain_gate).astype(low)
    grad_wout = lax.dot_general(
        normed_out, cot_low, (((0,), (0,)), ((), ())), preferred_element_type=f32
    )
    grad_gate = jnp.sum(d_out * gated * scale, 0)
    d_gated = scale * weighted - gated * (scale * scale * scale * inner_stat)
    d_y = (d_gated * gate_act).reshape(seqs, rows, heads, head_size)
    d_gate_in = (d_gated * y_all * sigma * (1.0 + gate_in * (1.0 - sigma))).astype(low)
    grad_wz = lax.dot_general(
        normed_low, d_gate_in, (((0,), (0,)), ((), ())), preferred_element_type=f32
    )
    sum_wout, sum_wz = lax.psum((grad_wout.astype(low), grad_wz.astype(low)), "ctx")
    sum_wout, sum_wz = sum_wout.astype(f32), sum_wz.astype(f32)

    dc_read, dgrowth_read, direct = read_back(d_y)
    carried = carry(decay, direct, False)
    d_decay = jnp.sum(carried * s_in, (2, 3))
    d_xheads, d_bmat, d_cmat, d_dtraw, grad_dtbias, grad_alog, grad_dskip = ssd_back(
        (d_y, dgrowth_read, d_decay, carried)
    )
    d_mixed = jnp.concatenate(
        [d_xheads.reshape(seqs, rows, inner), d_bmat, d_cmat + dc_read], -1
    )
    d_extended, grad_convw, grad_convb = conv_back(d_mixed)
    returned = shifted(d_extended[:, :edge], "ctx", -1)
    d_conv = d_extended[:, edge:]
    d_conv = jnp.concatenate(
        [d_conv[:, : rows - edge], d_conv[:, rows - edge :] + returned], 1
    )
    d_conv_low = d_conv.reshape(tokens, inner + maps).astype(low)
    d_dt_low = d_dtraw.reshape(tokens, heads).astype(low)
    nt = (((1,), (1,)), ((), ()))
    d_normed = lax.dot_general(d_conv_low, w_conv, nt, preferred_element_type=f32)
    d_normed = d_normed + lax.dot_general(d_gate_in, wz, nt, preferred_element_type=f32)
    d_normed = d_normed + lax.dot_general(d_dt_low, w_dt, nt, preferred_element_type=f32)
    grad_conv_all = lax.dot_general(
        normed_low, d_conv_low, (((0,), (0,)), ((), ())), preferred_element_type=f32
    )
    grad_wdt = lax.dot_general(
        normed_low, d_dt_low, (((0,), (0,)), ((), ())), preferred_element_type=f32
    )
    grad_wx, grad_wbc = grad_conv_all[:, :inner], grad_conv_all[:, inner:]

    tail = jnp.concatenate(
        [
            grad_wbc.astype(low).reshape(groups, -1),
            jnp.transpose(
                grad_convw[:, inner:].astype(low).reshape(taps, groups, -1), (1, 0, 2)
            ).reshape(groups, -1),
            grad_convb[inner:].astype(low).reshape(groups, -1),
        ],
        1,
    )
    tail_size = tail.shape[1]
    unit = width * 32
    tail = jnp.pad(tail, ((0, 0), (0, -(-tail_size // unit) * unit - tail_size)))
    token_half = own_rows // 2
    sends = jnp.concatenate(
        [
            d_normed.astype(low).reshape(groups, 2, token_half, width),
            tail.reshape(groups, 2, -1, width),
        ],
        2,
    )
    late_parts = (
        grad_wx,
        grad_wdt,
        grad_convw[:, :inner],
        grad_convb[:inner],
        grad_dtbias,
        grad_alog,
        grad_dskip,
        grad_gate,
    )
    blocks = lax.axis_size("ctx")
    small_late = pad_rows([part.astype(low) for part in late_parts[1:]], inner, 16 * blocks)
    late = jnp.concatenate([grad_wx.astype(low), small_late], 0)
    x_f = x_own.astype(f32)
    r1 = lax.rsqrt(jnp.mean(x_f * x_f, -1, keepdims=True) + EPSILON)
    scaled_x = (x_f * r1).reshape(2, token_half, width)
    got_d, late, bc_sum, gain_sum = finish(
        sends, late.reshape(blocks, -1, inner), scaled_x, token_half
    )
    d_normed_own = got_d.reshape(own_rows, width).astype(f32)
    b = d_normed_own * gain
    d_inputs = r1 * b - x_f * (r1 * r1 * r1) * jnp.mean(b * x_f, -1, keepdims=True)
    input_grad = (out_cotangent.reshape(own_rows, width).astype(f32) + d_inputs).reshape(
        seq_own, rows, width
    )
    late = late.reshape(-1, inner).astype(f32)
    sum_wx = late[:width]
    bc_sum = bc_sum.reshape(-1).astype(f32)
    sum_wdt, sum_convx, sum_biasx, sum_dtbias, sum_alog, sum_dskip, sum_gate = unpack(
        late[width:].reshape(-1), [part.shape for part in late_parts[1:]]
    )
    sum_wbc, sum_convbc, sum_biasbc = unpack(
        bc_sum, (w_bc.shape, conv_bc.shape, conv_bias_bc.shape)
    )
    gain_own = norm_gain.shape[0]
    sum_gain = lax.dynamic_slice_in_dim(gain_sum[0], own * gain_own, gain_own, 0)
    return (
        block_out.reshape(seq_own, rows, width),
        input_grad,
        sum_gain,
        jnp.stack([sum_wx, sum_wz], 1),
        sum_wbc,
        sum_wdt,
        sum_convx,
        sum_convbc,
        sum_biasx,
        sum_biasbc,
        sum_dtbias,
        sum_alog,
        sum_dskip,
        sum_gate,
        sum_wout,
    )


def solution(mesh):
    in_specs = (
        P("fsdp", "ctx", None),
        P("fsdp"),
        P(None, None, ("fsdp", "tp")),
        P("fsdp", None),
        P(None, ("fsdp", "tp")),
        P(None, ("fsdp", "tp")),
        P(None, "fsdp"),
        P(("fsdp", "tp")),
        P("fsdp"),
        P(("fsdp", "tp")),
        P(("fsdp", "tp")),
        P(("fsdp", "tp")),
        P(("fsdp", "tp")),
        P(("fsdp", "tp"), None),
        P("fsdp", "ctx", None),
    )
    out_specs = (
        P("fsdp", "ctx", None),
        P("fsdp", "ctx", None),
        P("fsdp"),
        P(None, None, ("fsdp", "tp")),
        P("fsdp", None),
        P(None, ("fsdp", "tp")),
        P(None, ("fsdp", "tp")),
        P(None, "fsdp"),
        P(("fsdp", "tp")),
        P("fsdp"),
        P(("fsdp", "tp")),
        P(("fsdp", "tp")),
        P(("fsdp", "tp")),
        P(("fsdp", "tp")),
        P(("fsdp", "tp"), None),
    )
    return jax.shard_map(body, mesh=mesh, in_specs=in_specs, out_specs=out_specs, check_vma=False)
```

```python
import functools

import jax
import jax.numpy as jnp
from jax import lax
from jax.experimental import pallas as pl
from jax.experimental.pallas import tpu as pltpu
from jax.sharding import PartitionSpec as P

EPSILON = 1e-05
PRECISE = lax.Precision.DEFAULT


def shifted(value, axis, steps):
    count = lax.axis_size(axis)
    initial, last = (max(0, -steps), min(count, count - steps))
    return lax.ppermute(value, axis, [(source, source + steps) for source in range(initial, last)])


def pre_norm(values, gain):
    mean_sq = jnp.mean(values * values, -1, keepdims=True)
    return values * lax.rsqrt(mean_sq + EPSILON) * gain


def conv_silu(extended, taps_w, taps_b):
    tap_count = taps_w.shape[0]
    out_rows = extended.shape[1] - tap_count + 1
    running = taps_b + extended[:, 0:out_rows] * taps_w[0]
    for offset in range(1, tap_count):
        running = running + extended[:, offset : offset + out_rows] * taps_w[offset]
    return jax.nn.silu(running)


def ssd_local(x_heads, b_mat, c_mat, dt_raw, dt_bias, a_log, d_skip):
    step_size = jax.nn.softplus(dt_raw + dt_bias)
    log_decay = -step_size * jnp.exp(a_log)
    upto = jnp.tril(jnp.ones((log_decay.shape[1],) * 2, jnp.float32))
    cumul = jnp.einsum("lm,smh->slh", upto, log_decay, precision=lax.Precision.HIGHEST)
    across = jnp.transpose(cumul, (0, 2, 1))
    step_t = jnp.transpose(step_size, (0, 2, 1))
    block_len = x_heads.shape[1]
    later_pos = lax.broadcasted_iota(jnp.int32, (block_len, block_len), 0)
    earlier_pos = lax.broadcasted_iota(jnp.int32, (block_len, block_len), 1)
    causal = later_pos >= earlier_pos
    gaps = across[:, :, :, None] - across[:, :, None, :]
    kernel = jnp.exp(jnp.where(causal, gaps, -1e30))
    scores = jnp.einsum("sln,smn->slm", c_mat, b_mat, precision=PRECISE)
    mixing = scores[:, None] * kernel * step_t[:, :, None, :]
    y_loc = (
        jnp.einsum("shlm,smhp->slhp", mixing, x_heads, precision=PRECISE)
        + d_skip[:, None] * x_heads
    )
    final = across[:, :, -1:]
    carry_w = jnp.exp(final - across) * step_t
    scaled = x_heads * jnp.transpose(carry_w, (0, 2, 1))[..., None]
    s_loc = jnp.einsum("slhp,sln->shpn", scaled, b_mat, precision=PRECISE)
    return (y_loc, jnp.exp(cumul), jnp.exp(final[..., 0]), s_loc)


def state_read(c_mat, growth, s_in):
    reading = jnp.einsum("sln,shpn->slhp", c_mat, s_in, precision=PRECISE)
    return growth[..., None] * reading


MESH = pl.DeviceIdType.MESH


def greet(peers):
    barrier = pltpu.get_barrier_semaphore()
    for peer in peers:
        pl.semaphore_signal(barrier, inc=1, device_id=peer, device_id_type=MESH)
    pl.semaphore_wait(barrier, len(peers))


def other(axis, steps):
    return {axis: lax.rem(lax.axis_index(axis) + steps, lax.axis_size(axis))}


def finish_kernel(
    groups,
    blocks,
    token_half,
    sends,
    late,
    scaled_x,
    branch,
    out_d,
    out_late,
    out_tail,
    out_gain,
    out_branch,
    pair_buf,
    pair_sum,
    row_buf,
    late_buf,
    acc,
    tail_own,
    tail_buf,
    gain_own,
    gain_buf,
    gain_rows,
    gain_row_buf,
    gain_pair,
    gain_pair_buf,
    pair_sems,
    row_sems,
    late_sems,
    spread_sems,
    tail_sems,
    gain_sems,
    gain_row_sems,
    last_sems,
):
    f32, low = jnp.float32, jnp.bfloat16
    own = lax.axis_index("fsdp")
    place = lax.axis_index("ctx")
    core = lax.axis_index("tp")
    partner = other("tp", 1)
    row_peers = [other("fsdp", k) for k in range(1, groups)]
    block_peers = [other("ctx", j) for j in range(1, blocks)]
    greet([partner] + row_peers + block_peers)

    def remote(source, target, sems, at, device):
        copy = pltpu.make_async_remote_copy(
            src_ref=source,
            dst_ref=target,
            send_sem=sems.at[0, at],
            recv_sem=sems.at[1, at],
            device_id=device,
            device_id_type=MESH,
        )
        copy.start()
        return copy

    order = list(range(1, groups)) + [0]
    pair = {}
    for k in order:
        row = lax.rem(own + k, groups)
        pair[k] = remote(sends.at[row, 1 - core], pair_buf.at[k], pair_sems, k, partner)
    lates = []
    for j in range(1, blocks):
        where = lax.rem(place + j, blocks)
        lates.append(remote(late.at[where], late_buf.at[j], late_sems, j, block_peers[j - 1]))
    rowc = []
    for k in order:
        row = lax.rem(own + k, groups)
        pair[k].wait_recv()
        total = sends[row, core].astype(f32) + pair_buf[k].astype(f32)
        if k:
            pair_sum[k] = total.astype(low)
            rowc.append(remote(pair_sum.at[k], row_buf.at[k], row_sems, k, row_peers[k - 1]))
        else:
            acc[...] = total
    out_branch[core] = branch[...]
    branch_copy = remote(out_branch.at[core], out_branch.at[core], last_sems, 3, partner)
    part = late[place].astype(f32)
    for j in range(1, blocks):
        lates[j - 1].wait_recv()
        part = part + late_buf[j].astype(f32)
    out_late[place] = part.astype(low)
    spread = []
    for j in range(1, blocks):
        spread.append(
            remote(out_late.at[place], out_late.at[place], spread_sems, j, block_peers[j - 1])
        )
    for k in range(1, groups):
        rowc[k - 1].wait_recv()
        acc[...] += row_buf[k].astype(f32)
    tail_own[...] = acc[token_half:].astype(low)
    tails = [
        remote(tail_own, tail_buf.at[j], tail_sems, j, block_peers[j - 1])
        for j in range(1, blocks)
    ]
    out_d[core] = acc[:token_half].astype(low)
    d_copy = remote(out_d.at[core], out_d.at[core], last_sems, 0, partner)
    gain = jnp.sum(acc[:token_half] * scaled_x[core], 0, keepdims=True)
    gain_own[...] = jnp.broadcast_to(gain, gain_own.shape)
    gains = [
        remote(gain_own, gain_buf.at[j], gain_sems, j, block_peers[j - 1])
        for j in range(1, blocks)
    ]
    gain = gain_own[...]
    for j in range(1, blocks):
        gains[j - 1].wait_recv()
        gain = gain + gain_buf[j]
    gain_rows[...] = gain
    gain_sent = [
        remote(gain_rows, gain_row_buf.at[k], gain_row_sems, k, row_peers[k - 1])
        for k in range(1, groups)
    ]
    tail = tail_own[...].astype(f32)
    for j in range(1, blocks):
        tails[j - 1].wait_recv()
        tail = tail + tail_buf[j].astype(f32)
    out_tail[core] = tail.astype(low)
    tail_copy = remote(out_tail.at[core], out_tail.at[core], last_sems, 1, partner)
    gain = gain_rows[...]
    for k in range(1, groups):
        gain_sent[k - 1].wait_recv()
        gain = gain + gain_row_buf[k]
    gain_pair[...] = gain
    gain_copy = remote(gain_pair, gain_pair_buf, last_sems, 2, partner)
    for copy in spread:
        copy.wait_recv()
    d_copy.wait_recv()
    tail_copy.wait_recv()
    branch_copy.wait_recv()
    gain_copy.wait_recv()
    out_gain[...] = gain_pair[...] + gain_pair_buf[...]
    everything = list(pair.values()) + lates + rowc + spread + tails + gains + gain_sent
    for copy in everything + [d_copy, tail_copy, gain_copy, branch_copy]:
        copy.wait_send()


def finish(sends, late, scaled_x, branch, token_half):
    groups, _, half, width = sends.shape
    blocks = late.shape[0]
    tail_half = half - token_half
    f32, low = jnp.float32, jnp.bfloat16
    vmem = pl.BlockSpec(memory_space=pltpu.VMEM)
    dma = pltpu.SemaphoreType.DMA
    return pl.pallas_call(
        functools.partial(finish_kernel, groups, blocks, token_half),
        out_shape=(
            jax.ShapeDtypeStruct((2, token_half, width), low),
            jax.ShapeDtypeStruct(late.shape, low),
            jax.ShapeDtypeStruct((2, tail_half, width), low),
            jax.ShapeDtypeStruct((8, width), f32),
            jax.ShapeDtypeStruct((2, token_half, width), low),
        ),
        in_specs=[vmem] * 4,
        out_specs=(vmem,) * 5,
        scratch_shapes=[
            pltpu.VMEM((groups, half, width), low),
            pltpu.VMEM((groups, half, width), low),
            pltpu.VMEM((groups, half, width), low),
            pltpu.VMEM(late.shape, low),
            pltpu.VMEM((half, width), f32),
            pltpu.VMEM((tail_half, width), low),
            pltpu.VMEM((blocks, tail_half, width), low),
            pltpu.VMEM((8, width), f32),
            pltpu.VMEM((blocks, 8, width), f32),
            pltpu.VMEM((8, width), f32),
            pltpu.VMEM((groups, 8, width), f32),
            pltpu.VMEM((8, width), f32),
            pltpu.VMEM((8, width), f32),
            dma((2, groups)),
            dma((2, groups)),
            dma((2, blocks)),
            dma((2, blocks)),
            dma((2, blocks)),
            dma((2, blocks)),
            dma((2, groups)),
            dma((2, 4)),
        ],
        compiler_params=pltpu.CompilerParams(
            collective_id=0, has_side_effects=True, vmem_limit_bytes=48 * 1024 * 1024
        ),
        cost_estimate=pl.CostEstimate(flops=10**7, bytes_accessed=10**8, transcendentals=0),
        name="finish",
    )(sends, late, scaled_x, branch)


def carry_kernel(
    blocks, forward, state, decay, out, state_buf, decay_buf, state_sems, decay_sems
):
    place = lax.axis_index("ctx")
    greet([other("ctx", j) for j in range(1, blocks)])
    hops = []
    for j in range(1, blocks):
        ahead, behind = place + j < blocks, place >= j
        sending, receiving = (ahead, behind) if forward else (behind, ahead)
        pair = [
            pltpu.make_async_remote_copy(
                src_ref=source,
                dst_ref=target.at[j],
                send_sem=sems.at[0, j],
                recv_sem=sems.at[1, j],
                device_id=other("ctx", j if forward else blocks - j),
                device_id_type=MESH,
            )
            for source, target, sems in (
                (state, state_buf, state_sems),
                (decay, decay_buf, decay_sems),
            )
        ]

        @pl.when(sending)
        def _():
            pair[0].start()
            pair[1].start()

        hops.append((j, pair, sending, receiving))
    out[...] = jnp.zeros_like(out)
    for j, pair, sending, receiving in hops[::-1]:

        @pl.when(receiving)
        def _():
            pair[0].wait_recv()
            pair[1].wait_recv()
            out[...] = decay_buf[j][:, None, :] * out[...] + state_buf[j].astype(jnp.float32)

    for j, pair, sending, receiving in hops:

        @pl.when(sending)
        def _():
            pair[0].wait_send()
            pair[1].wait_send()


def carry(decay, state, forward):
    seqs, heads, size, depth = state.shape
    blocks = lax.axis_size("ctx")
    pairs = seqs * heads
    low, f32 = jnp.bfloat16, jnp.float32
    vmem = pl.BlockSpec(memory_space=pltpu.VMEM)
    wide = jnp.broadcast_to(decay.reshape(pairs, 1), (pairs, depth))
    out = pl.pallas_call(
        functools.partial(carry_kernel, blocks, forward),
        out_shape=jax.ShapeDtypeStruct((pairs, size, depth), f32),
        in_specs=[vmem] * 2,
        out_specs=vmem,
        scratch_shapes=[
            pltpu.VMEM((blocks, pairs, size, depth), low),
            pltpu.VMEM((blocks, pairs, depth), f32),
            pltpu.SemaphoreType.DMA((2, blocks)),
            pltpu.SemaphoreType.DMA((2, blocks)),
        ],
        compiler_params=pltpu.CompilerParams(
            collective_id=1 if forward else 2,
            has_side_effects=True,
            vmem_limit_bytes=32 * 1024 * 1024,
        ),
        name="states" if forward else "state_grads",
    )(state.reshape(pairs, size, depth).astype(low), wide)
    return out.reshape(state.shape)


def stats_kernel(groups, cores, part, out, buf, sems):
    where = [
        (k, t) for k in range(groups) for t in range(cores) if k + t > 0
    ]
    peers = [{**other("fsdp", k), **other("tp", t)} for k, t in where]
    greet(peers)
    copies = []
    for at, peer in enumerate(peers):
        copy = pltpu.make_async_remote_copy(
            src_ref=part,
            dst_ref=buf.at[at],
            send_sem=sems.at[0, at],
            recv_sem=sems.at[1, at],
            device_id=peer,
            device_id_type=MESH,
        )
        copy.start()
        copies.append(copy)
    total = part[...]
    for at, copy in enumerate(copies):
        copy.wait_recv()
        total = total + buf[at]
    out[...] = total
    for copy in copies:
        copy.wait_send()


def stats_sum(part):
    groups, cores = lax.axis_size("fsdp"), lax.axis_size("tp")
    flat = part.reshape(-1, 128)
    vmem = pl.BlockSpec(memory_space=pltpu.VMEM)
    peers = groups * cores - 1
    out = pl.pallas_call(
        functools.partial(stats_kernel, groups, cores),
        out_shape=jax.ShapeDtypeStruct(flat.shape, flat.dtype),
        in_specs=[vmem],
        out_specs=vmem,
        scratch_shapes=[
            pltpu.VMEM((peers,) + flat.shape, flat.dtype),
            pltpu.SemaphoreType.DMA((2, peers)),
        ],
        compiler_params=pltpu.CompilerParams(collective_id=3, has_side_effects=True),
        name="token_stats",
    )(flat)
    return out.reshape(part.shape)


def pad_rows(parts, width, multiple):
    flat = jnp.concatenate([part.reshape(-1) for part in parts])
    unit = width * multiple
    total = -(-flat.shape[0] // unit) * unit
    return jnp.pad(flat, (0, total - flat.shape[0])).reshape(-1, width)


def unpack(flat, shapes):
    out, at = [], 0
    for shape in shapes:
        size = 1
        for n in shape:
            size *= n
        out.append(flat[..., at : at + size].reshape(flat.shape[:-1] + tuple(shape)))
        at += size
    return out


def gather_rows(x):
    half = x.shape[0] // lax.axis_size("tp")
    mine = lax.dynamic_slice_in_dim(x, lax.axis_index("tp") * half, half, 0)
    full = lax.all_gather(mine, ("fsdp", "tp"))
    return full.reshape((lax.axis_size("fsdp"),) + x.shape)


def body(
    block_input,
    norm_gain,
    w_xz,
    w_bc,
    w_dt,
    conv_x,
    conv_bc,
    conv_bias_x,
    conv_bias_bc,
    dt_bias,
    a_log,
    d_skip,
    gate_gain,
    w_out,
    out_cotangent,
):
    f32, low = jnp.float32, jnp.bfloat16
    groups = lax.axis_size("fsdp")
    own = lax.axis_index("fsdp")
    seq_own, rows, width = block_input.shape
    own_rows = seq_own * rows
    seqs = groups * seq_own
    tokens = seqs * rows
    inner = w_xz.shape[2]
    inner_total = inner * groups * lax.axis_size("tp")
    maps = w_bc.shape[1]
    state = maps // 2
    heads = w_dt.shape[1]
    head_size = inner // heads
    taps = conv_x.shape[0]
    edge = taps - 1

    small_shapes = (w_bc.shape, norm_gain.shape, conv_bc.shape, conv_bias_bc.shape)
    small = pad_rows((w_bc, norm_gain, conv_bc, conv_bias_bc), width, 32)
    x_own = block_input.reshape(own_rows, width)
    packed = gather_rows(jnp.concatenate([x_own, small], 0))
    cot_low = gather_rows(out_cotangent.reshape(own_rows, width)).reshape(tokens, width)
    x_all = packed[:, :own_rows].reshape(tokens, width).astype(f32)
    g_bc, g_gain, g_cbc, g_bbc = unpack(packed[:, own_rows:].reshape(groups, -1), small_shapes)
    wbc = g_bc.reshape(width, maps)
    gain = g_gain.reshape(width).astype(f32)
    convbc = jnp.transpose(g_cbc, (1, 0, 2)).reshape(taps, maps)
    biasbc = g_bbc.reshape(maps)

    normed_low = pre_norm(x_all, gain).astype(low)
    wx, wz = w_xz[:, 0], w_xz[:, 1]
    w_conv = jnp.concatenate([wx, wbc], 1)
    conv_low = jnp.dot(normed_low, w_conv, preferred_element_type=f32).astype(low)
    conv_low = conv_low.reshape(seqs, rows, inner + maps)
    gate_in = jnp.dot(normed_low, wz, preferred_element_type=f32)
    dt_raw = jnp.dot(normed_low, w_dt, preferred_element_type=f32)
    previous = shifted(conv_low[:, rows - edge :], "ctx", 1)
    extended = jnp.concatenate([previous, conv_low], 1).astype(f32)
    conv_w = jnp.concatenate([conv_x, convbc], -1).astype(f32)
    conv_b = jnp.concatenate([conv_bias_x, biasbc], -1).astype(f32)
    conv_out, conv_back = jax.vjp(conv_silu, extended, conv_w, conv_b)
    mixed = conv_out.astype(low).astype(f32)
    x_heads = mixed[..., :inner].reshape(seqs, rows, heads, head_size)
    b_mat = mixed[..., inner : inner + state]
    c_mat = mixed[..., inner + state :]
    local_out, ssd_back = jax.vjp(
        ssd_local,
        x_heads,
        b_mat,
        c_mat,
        dt_raw.reshape(seqs, rows, heads),
        dt_bias.astype(f32),
        a_log.astype(f32),
        d_skip.astype(f32),
    )
    y_loc, growth, decay, s_loc = local_out
    s_in = carry(decay, s_loc, True)
    y_off, read_back = jax.vjp(state_read, c_mat, growth, s_in)
    y_all = (y_loc + y_off).reshape(tokens, inner)
    sigma = jax.nn.sigmoid(gate_in)
    gate_act = gate_in * sigma
    gated = y_all * gate_act
    gain_gate = gate_gain.astype(f32)
    d_out = lax.dot_general(cot_low, w_out, (((1,), (1,)), ((), ())), preferred_element_type=f32)
    weighted = d_out * gain_gate
    stats = jnp.stack([jnp.sum(gated * gated, -1), jnp.sum(weighted * gated, -1)])
    stats = stats_sum(stats)
    scale = lax.rsqrt(stats[0] / inner_total + EPSILON)[:, None]
    inner_stat = stats[1][:, None] / inner_total
    branch = jnp.dot((gated * gain_gate).astype(low), w_out, preferred_element_type=f32)
    branch = lax.psum_scatter(
        branch.astype(low), ("fsdp", "tp"), scatter_dimension=0, tiled=True
    )
    scale_own = lax.dynamic_slice_in_dim(scale, own * own_rows, own_rows, 0)

    normed_out = (gated * scale * gain_gate).astype(low)
    grad_wout = lax.dot_general(
        cot_low, normed_out, (((0,), (0,)), ((), ())), preferred_element_type=f32
    )
    grad_gate = jnp.sum(d_out * gated * scale, 0)
    d_gated = scale * weighted - gated * (scale * scale * scale * inner_stat)
    d_y = (d_gated * gate_act).reshape(seqs, rows, heads, head_size)
    d_gate_in = (d_gated * y_all * sigma * (1.0 + gate_in * (1.0 - sigma))).astype(low)
    grad_wz = lax.dot_general(
        normed_low, d_gate_in, (((0,), (0,)), ((), ())), preferred_element_type=f32
    )
    dc_read, dgrowth_read, direct = read_back(d_y)
    carried = carry(decay, direct, False)
    d_decay = jnp.sum(carried * s_in, (2, 3))
    d_xheads, d_bmat, d_cmat, d_dtraw, grad_dtbias, grad_alog, grad_dskip = ssd_back(
        (d_y, dgrowth_read, d_decay, carried)
    )
    d_mixed = jnp.concatenate(
        [d_xheads.reshape(seqs, rows, inner), d_bmat, d_cmat + dc_read], -1
    )
    d_extended, grad_convw, grad_convb = conv_back(d_mixed)
    returned = shifted(d_extended[:, :edge], "ctx", -1)
    d_conv = d_extended[:, edge:]
    d_conv = jnp.concatenate(
        [d_conv[:, : rows - edge], d_conv[:, rows - edge :] + returned], 1
    )
    d_conv_low = d_conv.reshape(tokens, inner + maps).astype(low)
    d_dt_low = d_dtraw.reshape(tokens, heads).astype(low)
    nt = (((1,), (1,)), ((), ()))
    d_normed = lax.dot_general(d_conv_low, w_conv, nt, preferred_element_type=f32)
    d_normed = d_normed + lax.dot_general(d_gate_in, wz, nt, preferred_element_type=f32)
    d_normed = d_normed + lax.dot_general(d_dt_low, w_dt, nt, preferred_element_type=f32)
    grad_conv_all = lax.dot_general(
        normed_low, d_conv_low, (((0,), (0,)), ((), ())), preferred_element_type=f32
    )
    grad_wdt = lax.dot_general(
        normed_low, d_dt_low, (((0,), (0,)), ((), ())), preferred_element_type=f32
    )
    grad_wx, grad_wbc = grad_conv_all[:, :inner], grad_conv_all[:, inner:]

    tail = jnp.concatenate(
        [
            grad_wbc.astype(low).reshape(groups, -1),
            jnp.transpose(
                grad_convw[:, inner:].astype(low).reshape(taps, groups, -1), (1, 0, 2)
            ).reshape(groups, -1),
            grad_convb[inner:].astype(low).reshape(groups, -1),
        ],
        1,
    )
    tail_size = tail.shape[1]
    unit = width * 32
    tail = jnp.pad(tail, ((0, 0), (0, -(-tail_size // unit) * unit - tail_size)))
    token_half = own_rows // 2
    sends = jnp.concatenate(
        [
            d_normed.astype(low).reshape(groups, 2, token_half, width),
            tail.reshape(groups, 2, -1, width),
        ],
        2,
    )
    late_parts = (
        grad_wx,
        grad_wdt,
        grad_convw[:, :inner],
        grad_convb[:inner],
        grad_dtbias,
        grad_alog,
        grad_dskip,
        grad_gate,
    )
    blocks = lax.axis_size("ctx")
    small_late = pad_rows([part.astype(low) for part in late_parts[1:]], inner, 16 * blocks)
    large = [part.astype(low) for part in (grad_wx, grad_wz, grad_wout)]
    late = jnp.concatenate(large + [small_late], 0)
    x_f = x_own.astype(f32)
    r1 = lax.rsqrt(jnp.mean(x_f * x_f, -1, keepdims=True) + EPSILON)
    scaled_x = (x_f * r1).reshape(2, token_half, width)
    got_d, late, bc_sum, gain_sum, branch = finish(
        sends, late.reshape(blocks, -1, inner), scaled_x, branch, token_half
    )
    branch = branch.reshape(own_rows, width).astype(f32)
    block_out = (x_own.astype(f32) + branch * scale_own).astype(low)
    d_normed_own = got_d.reshape(own_rows, width).astype(f32)
    b = d_normed_own * gain
    d_inputs = r1 * b - x_f * (r1 * r1 * r1) * jnp.mean(b * x_f, -1, keepdims=True)
    input_grad = (out_cotangent.reshape(own_rows, width).astype(f32) + d_inputs).reshape(
        seq_own, rows, width
    )
    late = late.reshape(-1, inner).astype(f32)
    sum_wx, sum_wz = late[:width], late[width : 2 * width]
    sum_wout = late[2 * width : 3 * width].T
    bc_sum = bc_sum.reshape(-1).astype(f32)
    sum_wdt, sum_convx, sum_biasx, sum_dtbias, sum_alog, sum_dskip, sum_gate = unpack(
        late[3 * width :].reshape(-1), [part.shape for part in late_parts[1:]]
    )
    sum_wbc, sum_convbc, sum_biasbc = unpack(
        bc_sum, (w_bc.shape, conv_bc.shape, conv_bias_bc.shape)
    )
    gain_own = norm_gain.shape[0]
    sum_gain = lax.dynamic_slice_in_dim(gain_sum[0], own * gain_own, gain_own, 0)
    return (
        block_out.reshape(seq_own, rows, width),
        input_grad,
        sum_gain,
        jnp.stack([sum_wx, sum_wz], 1),
        sum_wbc,
        sum_wdt,
        sum_convx,
        sum_convbc,
        sum_biasx,
        sum_biasbc,
        sum_dtbias,
        sum_alog,
        sum_dskip,
        sum_gate,
        sum_wout,
    )


def solution(mesh):
    in_specs = (
        P("fsdp", "ctx", None),
        P("fsdp"),
        P(None, None, ("fsdp", "tp")),
        P("fsdp", None),
        P(None, ("fsdp", "tp")),
        P(None, ("fsdp", "tp")),
        P(None, "fsdp"),
        P(("fsdp", "tp")),
        P("fsdp"),
        P(("fsdp", "tp")),
        P(("fsdp", "tp")),
        P(("fsdp", "tp")),
        P(("fsdp", "tp")),
        P(("fsdp", "tp"), None),
        P("fsdp", "ctx", None),
    )
    out_specs = (
        P("fsdp", "ctx", None),
        P("fsdp", "ctx", None),
        P("fsdp"),
        P(None, None, ("fsdp", "tp")),
        P("fsdp", None),
        P(None, ("fsdp", "tp")),
        P(None, ("fsdp", "tp")),
        P(None, "fsdp"),
        P(("fsdp", "tp")),
        P("fsdp"),
        P(("fsdp", "tp")),
        P(("fsdp", "tp")),
        P(("fsdp", "tp")),
        P(("fsdp", "tp")),
        P(("fsdp", "tp"), None),
    )
    return jax.shard_map(body, mesh=mesh, in_specs=in_specs, out_specs=out_specs, check_vma=False)
```
